256 devices in a mesh: pos: 8 (over y, x_lo), head: 8 (over z), rep: 4 (over x_hi, core).
Axes of the slice: x: 4 (x_hi: 2, x_lo: 2; x = x_hi * 2 + x_lo), y: 4, z: 8, core: 2. Of those that a mesh axis runs over, the one named last changes fastest.
Arguments:
- queries: bfloat16 [2048, 64, 128], P(('pos', 'rep'), 'head'), may hold values from -5 to 5
- doc_keys: bfloat16 [32768, 8, 128], P('pos', 'head'), may hold values from -4.5 to 4.5
- doc_values: bfloat16 [32768, 8, 128], P('pos', 'head'), may hold values from -6 to 6
- suffix_keys: bfloat16 [2048, 128, 8, 128], P(('pos', 'rep'), None, 'head'), may hold values from -10 to 10
- suffix_values: bfloat16 [2048, 128, 8, 128], P(('pos', 'rep'), None, 'head'), may hold values from -6 to 6
- suffix_len: int32 [2048], P(('pos', 'rep')), may hold values from 1 to 128, as said below
- out_weight: bfloat16 [8192, 8192], P('head', ('pos', 'rep')), may hold values from -0.25 to 0.25
Outputs:
- projected: bfloat16 [2048, 8192], P(None, ('pos', 'rep'))
The draws below stay inside these ranges and needn't reach their ends.
Inputs may be any that keep to these rules, and one draw needn't show every extreme that they name: `suffix_len`: the last live private position holds the new token's key and value.
All inputs are finite; a program needn't handle non-finite values.
Results may differ from the reference program's by a relative error of at most 0.02.
Values may be sent and summed in bfloat16 or wider, within the bound.
No kernel may reach another device: no remote copies, remote signals or barrier semaphores. Data moves between devices by JAX's collectives and lax.ppermute only.
A program may use at most 192 MiB of HBM per device.

```python
import jax
import jax.numpy as jnp
from jax import lax

D = 8192
HQ = 64
KVH = 8
HEAD_DIM = 128
SUFFIX_SLOTS = 128
DOC = 32768
REQ = 2048
N_POS = 8


def draw_queries(key, part):
    key = jax.random.fold_in(key, 11)
    base = jnp.clip(1.2 * jax.random.normal(key, (REQ, HQ, HEAD_DIM), jnp.float32), -5.0, 5.0)
    return base.astype(jnp.bfloat16)


def draw_doc_keys(key, part):
    key = jax.random.fold_in(key, 23)
    base = jnp.clip(jax.random.normal(key, (DOC, KVH, HEAD_DIM), jnp.float32), -4.5, 4.5)
    return base.astype(jnp.bfloat16)


def draw_suffix_len(key, part):
    key = jax.random.fold_in(key, 37)
    key_len, key_spot = jax.random.split(key)
    lengths = jax.random.randint(key_len, (REQ,), 1, SUFFIX_SLOTS + 1)
    spot = jax.random.randint(key_spot, (), 0, REQ)
    return lengths.at[spot].set(SUFFIX_SLOTS).astype(jnp.int32)


def block_scale(key, extent, pieces, smallest, top_value):
    gain = 1.0
    for position, shards_of in pieces:
        draws = jax.random.uniform(jax.random.fold_in(jax.random.fold_in(key, 6), position), (shards_of,), jnp.float32, smallest / len(pieces), top_value / len(pieces))
        gain = gain * jnp.repeat(jnp.exp(draws), extent[position] // shards_of).reshape((-1,) + (1,) * (len(extent) - 1 - position))
    return gain


def centred(own_key, dims, deviation, limit, cuts=(), kind=jnp.bfloat16):
    values = jax.random.normal(own_key, dims, jnp.float32) * deviation
    if len(cuts) > 0:
        values = block_scale(own_key, dims, cuts, -0.22, 0.18) * values
    return jnp.clip(values, min=-limit, max=limit).astype(kind)


def setup_inputs(seed: int = 0) -> dict:
    key_list = jax.random.split(jax.random.key(seed), 8)
    queries = draw_queries(jax.random.fold_in(key_list[7], 71), 0)
    doc_keys = draw_doc_keys(jax.random.fold_in(key_list[7], 71), 0)
    doc_values = centred(key_list[2], (DOC, KVH, HEAD_DIM), 1.0, 6.0, ((0, 8), (1, 8)))
    suffix_keys = centred(key_list[3], (REQ, SUFFIX_SLOTS, KVH, HEAD_DIM), 2.5, 10.0, ((0, 32), (2, 8)))
    suffix_values = centred(key_list[4], (REQ, SUFFIX_SLOTS, KVH, HEAD_DIM), 1.0, 6.0, ((0, 32), (2, 8)))
    suffix_len = draw_suffix_len(jax.random.fold_in(key_list[7], 71), 0)
    out_weight = centred(key_list[6], (HQ * HEAD_DIM, D), (HQ * HEAD_DIM // 16) ** -0.5, 0.25, ((0, 8), (1, 32)))
    return {"queries": queries, "doc_keys": doc_keys, "doc_values": doc_values, "suffix_keys": suffix_keys, "suffix_values": suffix_values, "suffix_len": suffix_len, "out_weight": out_weight}


def reference(queries, doc_keys, doc_values, suffix_keys, suffix_values, suffix_len, out_weight):
    group = HQ // KVH
    score_scale = HEAD_DIM ** -0.5
    block_list = N_POS
    block_row_count = REQ // block_list
    query_all = queries.astype(jnp.float32).reshape(REQ, KVH, group, HEAD_DIM).transpose(1, 0, 2, 3)
    key_doc = doc_keys.astype(jnp.float32).transpose(1, 0, 2)
    value_doc = doc_values.astype(jnp.float32).transpose(1, 0, 2)
    key_suf = suffix_keys.astype(jnp.float32).transpose(2, 0, 1, 3)
    value_suf = suffix_values.astype(jnp.float32).transpose(2, 0, 1, 3)
    live = jnp.arange(SUFFIX_SLOTS, dtype=jnp.int32)[None, :] < suffix_len[:, None]
    live_blocks = live.reshape(block_list, block_row_count, SUFFIX_SLOTS)

    def one_head(input_arrays):
        query_head_slice, key_head_slice, value_head_slice, suffix_key_head, suffix_value_head = input_arrays

        def one_block(part_results):
            query_row_set, suffix_key_rows, suffix_value_rows, active_mask = part_results
            doc_scores = jnp.einsum("rgd,sd->rgs", query_row_set, key_head_slice) * score_scale
            suffix_logits = jnp.einsum("umb,uab->uma", query_row_set, suffix_key_rows) * score_scale
            alive_b = active_mask[:, None, :]
            masked = jnp.where(alive_b, suffix_logits, -1e30)
            top = jnp.maximum(doc_scores.max(-1), masked.max(-1))
            doc_terms = jnp.exp(doc_scores - top[..., None])
            suffix_terms = jnp.where(alive_b, jnp.exp(masked - top[..., None]), 0.0)
            total = doc_terms.sum(-1) + suffix_terms.sum(-1)
            doc_weights = lax.optimization_barrier(doc_terms.astype(jnp.bfloat16)).astype(jnp.float32)
            suffix_weights = lax.optimization_barrier(suffix_terms.astype(jnp.bfloat16)).astype(jnp.float32)
            summed = jnp.einsum("rgs,sd->rgd", doc_weights, value_head_slice) + jnp.einsum("rgj,rjd->rgd", suffix_weights, suffix_value_rows)
            return (summed / total[..., None]).astype(jnp.bfloat16)

        outs = lax.map(one_block, (query_head_slice.reshape(block_list, block_row_count, group, HEAD_DIM),
                                   suffix_key_head.reshape(block_list, block_row_count, SUFFIX_SLOTS, HEAD_DIM),
                                   suffix_value_head.reshape(block_list, block_row_count, SUFFIX_SLOTS, HEAD_DIM),
                                   live_blocks))
        return outs.reshape(REQ, group, HEAD_DIM)

    attended = lax.map(one_head, (query_all, key_doc, value_doc, key_suf, value_suf))
    attended = attended.transpose(1, 0, 2, 3).reshape(REQ, HQ * HEAD_DIM)
    product = jnp.dot(attended.astype(jnp.float32), out_weight.astype(jnp.float32), preferred_element_type=jnp.float32)
    return product.astype(jnp.bfloat16)
```

```python
import functools
import math

import jax
import jax.numpy as jnp
from jax import lax
from jax.experimental import pallas as pl
from jax.experimental.pallas import tpu as pltpu
from jax.sharding import PartitionSpec as P

BF = jnp.bfloat16
F32 = jnp.float32
LOG2E = math.log2(math.e)
VMEM = 48 * 2**20
KEY_TILE = 512
MSG_ROWS = 144


def params():
    return pltpu.CompilerParams(vmem_limit_bytes=VMEM)


def whole(shape):
    return pl.BlockSpec(shape, lambda *_: (0,) * len(shape))


def doc_kernel(q_ref, k_ref, v_ref, out_ref, vt_ref):
    n_keys, head_size = k_ref.shape
    tiles = n_keys // KEY_TILE

    @pl.when(pl.program_id(0) == 0)
    def _():
        for j in range(tiles):
            span = pl.ds(j * KEY_TILE, KEY_TILE)
            vt_ref[pl.ds(0, head_size), span] = v_ref[span, :].T
        vt_ref[pl.ds(head_size, 16), :] = jnp.ones((16, n_keys), BF)

    q = q_ref[0]

    def scores(j):
        return lax.dot_general(
            k_ref[pl.ds(j * KEY_TILE, KEY_TILE), :],
            q,
            (((1,), (1,)), ((), ())),
            preferred_element_type=F32,
        )

    def mix(j, s, shift):
        weights = jnp.exp2(s - shift).astype(BF)
        return jnp.dot(
            vt_ref[:, pl.ds(j * KEY_TILE, KEY_TILE)], weights, preferred_element_type=F32
        )

    def emit(acc, shift):
        total = acc[head_size : head_size + 1]
        lse = shift + jnp.log2(total)
        high = lse.astype(BF).astype(F32)
        mid = (lse - high).astype(BF).astype(F32)
        low = lse - high - mid
        out_ref[0, pl.ds(0, head_size), :] = (acc[:head_size] / total).astype(BF)
        row = lax.broadcasted_iota(jnp.int32, (16, q.shape[0]), 0)
        tail = jnp.where(row == 0, high, jnp.where(row == 1, mid, jnp.where(row == 2, low, 0.0)))
        out_ref[0, pl.ds(head_size, 16), :] = tail.astype(BF)

    s = scores(0)
    shift = s.max(0, keepdims=True)
    acc = None
    for j in range(tiles):
        ahead = scores(j + 1) if j + 1 < tiles else None
        part = mix(j, s, shift)
        acc = part if acc is None else acc + part
        s = ahead
    emit(acc, shift)
    worst = jnp.max(jnp.where(acc[head_size : head_size + 1] < 1e30, 0.0, 1.0))

    @pl.when(worst > 0.5)
    def _():
        def largest(j, top):
            return jnp.maximum(top, scores(j).max(0, keepdims=True))

        top = lax.fori_loop(1, tiles, largest, shift)

        def again(j, total):
            s_j = lax.dot_general(
                k_ref[pl.ds(pl.multiple_of(j * KEY_TILE, KEY_TILE), KEY_TILE), :],
                q,
                (((1,), (1,)), ((), ())),
                preferred_element_type=F32,
            )
            weights = jnp.exp2(s_j - top).astype(BF)
            return total + jnp.dot(
                vt_ref[:, pl.ds(pl.multiple_of(j * KEY_TILE, KEY_TILE), KEY_TILE)],
                weights,
                preferred_element_type=F32,
            )

        emit(lax.fori_loop(0, tiles, again, jnp.zeros(acc.shape, F32)), top)


def doc_attention(q_all, keys, values):
    n_src, rows, head_size = q_all.shape
    n_keys = keys.shape[0]
    work = n_src * rows * n_keys
    return pl.pallas_call(
        doc_kernel,
        grid=(n_src,),
        in_specs=[
            pl.BlockSpec((1, rows, head_size), lambda i: (i, 0, 0)),
            whole((n_keys, head_size)),
            whole((n_keys, head_size)),
        ],
        out_specs=pl.BlockSpec((1, MSG_ROWS, rows), lambda i: (i, 0, 0)),
        out_shape=jax.ShapeDtypeStruct((n_src, MSG_ROWS, rows), BF),
        scratch_shapes=[pltpu.VMEM((MSG_ROWS, n_keys), BF)],
        compiler_params=params(),
        cost_estimate=pl.CostEstimate(
            flops=4 * work * head_size, bytes_accessed=2**22, transcendentals=work
        ),
        name="doc_attention",
    )(q_all, keys, values)


def suffix_kernel(scale, step, len_ref, q_ref, k_ref, v_ref, out_ref, lse_ref):
    base = pl.program_id(0) * step
    slots = k_ref.shape[1]
    lane = lax.broadcasted_iota(jnp.int32, (8, slots), 1)
    scored = [
        lax.dot_general(
            q_ref[i], k_ref[i], (((1,), (1,)), ((), ())), preferred_element_type=F32
        )
        for i in range(step)
    ]
    for i in range(step):
        live = lane < len_ref[base + i]
        s = jnp.where(live, scored[i] * scale, -1e30)
        top = s.max(1, keepdims=True)
        terms = jnp.where(live, jnp.exp2(s - top), 0.0)
        total = terms.sum(1, keepdims=True)
        mixed = jnp.dot(terms.astype(BF), v_ref[i], preferred_element_type=F32) / total
        place = pl.ds((i // 8) * 64 + i % 8, 8, stride=8)
        out_ref[place, :] = mixed
        lse_ref[place, :] = jnp.broadcast_to(top + jnp.log2(total), mixed.shape)


def suffix_attention(queries, keys, values, lens):
    n_req, heads, head_size = queries.shape
    slots = keys.shape[1]
    step = 16
    rows = step * heads
    scale = head_size ** (-0.5) * LOG2E
    wide = jax.ShapeDtypeStruct((n_req * heads, head_size), F32)
    return pl.pallas_call(
        functools.partial(suffix_kernel, scale, step),
        grid=(n_req // step,),
        in_specs=[
            pl.BlockSpec(memory_space=pltpu.SMEM),
            pl.BlockSpec((step, heads, head_size), lambda i: (i, 0, 0)),
            pl.BlockSpec((step, slots, head_size), lambda i: (i, 0, 0)),
            pl.BlockSpec((step, slots, head_size), lambda i: (i, 0, 0)),
        ],
        out_specs=[pl.BlockSpec((rows, head_size), lambda i: (i, 0))] * 2,
        out_shape=[wide, wide],
        compiler_params=params(),
        cost_estimate=pl.CostEstimate(
            flops=4 * n_req * heads * slots * head_size, bytes_accessed=2**22, transcendentals=2**16
        ),
        name="suffix_attention",
    )(lens, queries, keys, values)


def combine_kernel(head_size, msg_ref, own_ref, own_lse_ref, out_ref):
    n_src, _, rows = msg_ref.shape
    lses = []
    for i in range(n_src):
        tail = msg_ref[i, pl.ds(head_size, 16), :].astype(F32)
        lses.append(tail[0:1] + tail[1:2] + tail[2:3])
    top = functools.reduce(jnp.maximum, lses)
    total = None
    acc = None
    for i in range(n_src):
        w = jnp.exp2(lses[i] - top)
        part = msg_ref[i, pl.ds(0, head_size), :].astype(F32) * w
        total = w if total is None else total + w
        acc = part if acc is None else acc + part
    doc = (acc / total).T
    doc_lse = jnp.broadcast_to(top + jnp.log2(total), (head_size, rows)).T
    own_lse = own_lse_ref[...]
    peak = jnp.maximum(doc_lse, own_lse)
    w_doc = jnp.exp2(doc_lse - peak)
    w_own = jnp.exp2(own_lse - peak)
    out_ref[...] = ((doc * w_doc + own_ref[...] * w_own) / (w_doc + w_own)).astype(BF)


def combine(msgs, own, own_lse):
    rows, head_size = own.shape
    return pl.pallas_call(
        functools.partial(combine_kernel, head_size),
        out_shape=jax.ShapeDtypeStruct((rows, head_size), BF),
        compiler_params=params(),
        name="combine",
    )(msgs, own, own_lse)


def project_kernel(steps, *refs):
    first, second = refs[0:4], refs[4:8]
    w_ref, w_far_ref, out_ref, far_ref, acc_ref, acc_far_ref = refs[8:]
    h = pl.program_id(0)

    @pl.when(h == 0)
    def _():
        acc_ref[...] = jnp.zeros_like(acc_ref)
        acc_far_ref[...] = jnp.zeros_like(acc_far_ref)

    def add(pieces):
        cols = []
        for j in range(8):
            rows = jnp.concatenate([piece(j).astype(F32) for piece in pieces], 0)
            cols.append(rows.reshape(-1, 128).astype(BF))
        lhs = jnp.concatenate(cols, 1)
        acc_ref[...] += jnp.dot(lhs, w_ref[...], preferred_element_type=F32)
        acc_far_ref[...] += jnp.dot(lhs, w_far_ref[...], preferred_element_type=F32)

    @pl.when(h < steps // 2)
    def _():
        add([lambda j, dx=dx: first[dx][:, h * 8 + j] for dx in range(4)])

    @pl.when(h >= steps // 2)
    def _():
        add(
            [
                lambda j, dx=dx, dy=dy: second[dy][pl.ds(dx, 1), (h - steps // 2) * 8 + j]
                for dx in range(4)
                for dy in range(4)
            ]
        )

    @pl.when(h == steps - 1)
    def _():
        out_ref[...] = acc_ref[...].astype(BF)
        far_ref[...] = acc_far_ref[...].astype(BF)


def project(first, second, w, w_far):
    steps = 8
    depth = w.shape[0] // steps
    cols = w.shape[1]
    rows = 128
    piece = first[0].shape
    return pl.pallas_call(
        functools.partial(project_kernel, steps),
        grid=(steps,),
        in_specs=[whole(piece)] * 8 + [pl.BlockSpec((depth, cols), lambda i: (i, 0))] * 2,
        out_specs=[whole((rows, cols))] * 2,
        out_shape=[jax.ShapeDtypeStruct((rows, cols), BF)] * 2,
        scratch_shapes=[pltpu.VMEM((rows, cols), F32)] * 2,
        compiler_params=params(),
        cost_estimate=pl.CostEstimate(
            flops=4 * rows * w.shape[0] * cols, bytes_accessed=10 * 2**20, transcendentals=0
        ),
        name="project",
    )(*first, *second, w, w_far)


def place_kernel(where_ref, *refs):
    out_ref = refs[-1]
    y, x, core, z = where_ref[0], where_ref[1], where_ref[2], where_ref[3]
    for s in range(8):
        layer = lax.rem(z + 8 - s, 8)
        for c in range(2):
            src = refs[2 * s + c]
            at_core = core if c == 0 else 1 - core
            for dx in range(4):
                sx = lax.rem(x + 4 - dx, 4)
                for dy in range(4):
                    sy = lax.rem(y + 4 - dy, 4)
                    pos = sy * 2 + lax.rem(sx, 2)
                    rep = (sx // 2) * 2 + at_core
                    out_ref[pos, rep, layer] = src[dx * 4 + dy]


def place(where, pieces, cols):
    return pl.pallas_call(
        place_kernel,
        in_specs=[pl.BlockSpec(memory_space=pltpu.SMEM)] + [whole((16, 8, cols))] * len(pieces),
        out_specs=whole((8, 4, 8, 8, cols)),
        out_shape=jax.ShapeDtypeStruct((8, 4, 8, 8, cols), BF),
        compiler_params=params(),
        name="place",
    )(where, *[p.reshape(16, 8, cols) for p in pieces])


def plane_shift(value, dy, dx):
    pairs = []
    for pos in range(8):
        for rep in range(4):
            y, x, core = pos // 2, (rep // 2) * 2 + pos % 2, rep % 2
            ty, tx = (y + dy) % 4, (x + dx) % 4
            pairs.append((pos * 4 + rep, (ty * 2 + tx % 2) * 4 + (tx // 2) * 2 + core))
    return lax.ppermute(value, ("pos", "rep"), pairs)


def head_shift(value, s):
    return lax.ppermute(value, "head", [(i, (i + s) % 8) for i in range(8)])


def other_core(value):
    return lax.ppermute(value, "rep", [(i, i ^ 1) for i in range(4)])


def body(queries, doc_keys, doc_values, suffix_keys, suffix_values, suffix_len, out_weight):
    n_req, heads, head_size = queries.shape
    keys = doc_keys.reshape(-1, head_size)
    values = doc_values.reshape(-1, head_size)
    s_keys = suffix_keys.reshape(n_req, -1, head_size)
    s_values = suffix_values.reshape(n_req, -1, head_size)
    n_pos = lax.axis_size("pos")

    w_near = lax.all_gather(out_weight, "head", axis=0, tiled=True)
    w_far = other_core(w_near)

    scaled = (queries.astype(F32) * (head_size ** (-0.5) * LOG2E)).astype(BF)
    ordered = scaled.reshape(8, 8, heads, head_size).transpose(0, 2, 1, 3)
    ordered = ordered.reshape(n_req * heads, head_size)
    q_all = lax.all_to_all(
        jnp.broadcast_to(ordered[None], (n_pos,) + ordered.shape), "pos", 0, 0, tiled=True
    )
    own, own_lse = suffix_attention(queries, s_keys, s_values, suffix_len)
    msgs = doc_attention(q_all, keys, values)
    msgs = lax.all_to_all(msgs, "pos", 0, 0, tiled=True)
    attended = combine(msgs, own, own_lse)

    rows = lax.all_to_all(attended.reshape(8, 64, head_size), "head", 0, 0, tiled=True)
    rows = rows.reshape(64, 8, head_size)
    half_a, half_b = rows[:32], rows[32:]
    along_y = jnp.stack([half_a] + [plane_shift(half_a, s, 0) for s in (1, 2, 3)])
    along_x = jnp.stack([half_b] + [plane_shift(half_b, 0, s) for s in (1, 2, 3)])
    first = [along_y] + [plane_shift(along_y, 0, s) for s in (1, 2, 3)]
    second = [along_x] + [plane_shift(along_x, s, 0) for s in (1, 2, 3)]
    near, far = project(first, second, w_near, w_far)
    far = other_core(far)

    pieces = [near, far]
    both = jnp.stack([near, far])
    for s in range(1, 8):
        got = head_shift(both, s)
        pieces += [got[0], got[1]]
    pos, rep, z = lax.axis_index("pos"), lax.axis_index("rep"), lax.axis_index("head")
    where = jnp.stack([pos // 2, (rep // 2) * 2 + pos % 2, rep % 2, z]).astype(jnp.int32)
    cols = out_weight.shape[1]
    return place(where, pieces, cols).reshape(-1, cols)


def solution(mesh):
    in_specs = (
        P(("pos", "rep"), "head", None),
        P("pos", "head", None),
        P("pos", "head", None),
        P(("pos", "rep"), None, "head", None),
        P(("pos", "rep"), None, "head", None),
        P(("pos", "rep")),
        P("head", ("pos", "rep")),
    )
    out_specs = P(None, ("pos", "rep"))
    return jax.shard_map(body, mesh=mesh, in_specs=in_specs, out_specs=out_specs, check_vma=False)
```

```python
import functools
import math

import jax
import jax.numpy as jnp
from jax import lax
from jax.experimental import pallas as pl
from jax.experimental.pallas import tpu as pltpu
from jax.sharding import PartitionSpec as P

BF = jnp.bfloat16
F32 = jnp.float32
LOG2E = math.log2(math.e)
VMEM = 32 * 2**20
FULL_VMEM = 56 * 2**20
KEY_TILE = 512
MSG_ROWS = 144


def params(limit=VMEM):
    return pltpu.CompilerParams(vmem_limit_bytes=limit)


def whole(shape):
    return pl.BlockSpec(shape, lambda *_: (0,) * len(shape))


def transpose_kernel(v_ref, vt_ref):
    n_keys, head_size = v_ref.shape
    for j in range(n_keys // KEY_TILE):
        span = pl.ds(j * KEY_TILE, KEY_TILE)
        vt_ref[pl.ds(0, head_size), span] = v_ref[span, :].T
    vt_ref[pl.ds(head_size, 16), :] = jnp.ones((16, n_keys), BF)


def transpose_values(values):
    n_keys = values.shape[0]
    return pl.pallas_call(
        transpose_kernel,
        out_shape=jax.ShapeDtypeStruct((MSG_ROWS, n_keys), BF),
        compiler_params=params(),
        name="transpose_values",
    )(values)


def attend(q, k_ref, vt_ref, out_ref):
    n_keys, head_size = k_ref.shape
    tiles = n_keys // KEY_TILE

    def scores(j):
        return lax.dot_general(
            k_ref[pl.ds(pl.multiple_of(j * KEY_TILE, KEY_TILE), KEY_TILE), :],
            q,
            (((1,), (1,)), ((), ())),
            preferred_element_type=F32,
        )

    def mix(j, s, shift):
        weights = jnp.exp2(s - shift).astype(BF)
        span = pl.ds(pl.multiple_of(j * KEY_TILE, KEY_TILE), KEY_TILE)
        return jnp.dot(vt_ref[:, span], weights, preferred_element_type=F32)

    def emit(acc, shift):
        total = acc[head_size : head_size + 1]
        out_ref[pl.ds(0, head_size), :] = (acc[:head_size] / total).astype(BF)
        out_ref[pl.ds(head_size, 16), :] = split_lse(shift + jnp.log2(total), q.shape[0])

    s = scores(0)
    shift = s.max(0, keepdims=True)
    acc = None
    for j in range(tiles):
        ahead = scores(j + 1) if j + 1 < tiles else None
        part = mix(j, s, shift)
        acc = part if acc is None else acc + part
        s = ahead
    emit(acc, shift)
    worst = jnp.max(jnp.where(acc[head_size : head_size + 1] < 1e30, 0.0, 1.0))

    @pl.when(worst > 0.5)
    def _():
        top = lax.fori_loop(
            1, tiles, lambda j, top: jnp.maximum(top, scores(j).max(0, keepdims=True)), shift
        )
        again = lax.fori_loop(
            0, tiles, lambda j, total: total + mix(j, scores(j), top), jnp.zeros(acc.shape, F32)
        )
        emit(again, top)


def doc_kernel(q_ref, k_ref, vt_ref, *refs):
    out_ref = refs[-1]
    for i in range(q_ref.shape[0]):
        attend(q_ref[i], k_ref, vt_ref, out_ref.at[i])


def doc_attention(chunks, keys, vt, after=()):
    n, rows, head_size = chunks.shape
    n_keys = keys.shape[0]
    work = n * rows * n_keys
    vm = pl.BlockSpec(memory_space=pltpu.VMEM)
    return pl.pallas_call(
        doc_kernel,
        in_specs=[vm] * 3 + [pl.BlockSpec(memory_space=pl.ANY)] * len(after),
        out_specs=vm,
        out_shape=jax.ShapeDtypeStruct((n, MSG_ROWS, rows), BF),
        compiler_params=params(),
        cost_estimate=pl.CostEstimate(
            flops=10 * work * head_size, bytes_accessed=2**19, transcendentals=0
        ),
        name="doc_attention",
    )(chunks, keys, vt, *after)


def pair_kernel(a_ref, b_ref, after_ref, out_ref):
    out_ref[0] = a_ref[...]
    out_ref[1] = b_ref[...]


def pair_up(a, b, after):
    vm = pl.BlockSpec(memory_space=pltpu.VMEM)
    return pl.pallas_call(
        pair_kernel,
        in_specs=[vm, vm, pl.BlockSpec(memory_space=pl.ANY)],
        out_specs=vm,
        out_shape=jax.ShapeDtypeStruct((2,) + a.shape, a.dtype),
        compiler_params=params(),
        name="pair_up",
    )(a, b, after)


def suffix_kernel(scale, step, len_ref, q_ref, k_hbm, v_hbm, out_ref, lse_ref, k_ref, v_ref, sems):
    n_req, slots, _ = k_hbm.shape
    steps = n_req // step
    copies = []
    for g in range(steps):
        span = pl.ds(g * step, step)
        for i, (src, dst) in enumerate(((k_hbm, k_ref), (v_hbm, v_ref))):
            copies.append(pltpu.make_async_copy(src.at[span], dst.at[span], sems.at[i, g]))
            copies[-1].start()
    lane = lax.broadcasted_iota(jnp.int32, (8, slots), 1)
    for g in range(steps):
        copies[2 * g].wait()
        copies[2 * g + 1].wait()
        scored = [
            lax.dot_general(
                q_ref[r], k_ref[r], (((1,), (1,)), ((), ())), preferred_element_type=F32
            )
            for r in range(g * step, (g + 1) * step)
        ]
        for i in range(step):
            r = g * step + i
            live = lane < len_ref[r]
            s = jnp.where(live, scored[i] * scale, -1e30)
            top = s.max(1, keepdims=True)
            terms = jnp.where(live, jnp.exp2(s - top), 0.0)
            total = terms.sum(1, keepdims=True)
            mixed = jnp.dot(terms.astype(BF), v_ref[r], preferred_element_type=F32) / total
            place = pl.ds((r // 8) * 64 + r % 8, 8, stride=8)
            out_ref[place, :] = mixed
            lse_ref[place, :] = jnp.broadcast_to(top + jnp.log2(total), mixed.shape)


def suffix_attention(queries, keys, values, lens):
    n_req, heads, head_size = queries.shape
    step = 8
    scale = head_size ** (-0.5) * LOG2E
    wide = jax.ShapeDtypeStruct((n_req * heads, head_size), F32)
    vm = pl.BlockSpec(memory_space=pltpu.VMEM)
    hbm = pl.BlockSpec(memory_space=pl.ANY)
    return pl.pallas_call(
        functools.partial(suffix_kernel, scale, step),
        in_specs=[pl.BlockSpec(memory_space=pltpu.SMEM), vm, hbm, hbm],
        out_specs=[vm, vm],
        out_shape=[wide, wide],
        scratch_shapes=[
            pltpu.VMEM(keys.shape, BF),
            pltpu.VMEM(keys.shape, BF),
            pltpu.SemaphoreType.DMA((2, n_req // step)),
        ],
        compiler_params=params(FULL_VMEM),
        cost_estimate=pl.CostEstimate(
            flops=2 * 10**9, bytes_accessed=2**22, transcendentals=2**16
        ),
        name="suffix_attention",
    )(lens, queries, keys, values)


def split_lse(lse, width):
    high = lse.astype(BF).astype(F32)
    mid = (lse - high).astype(BF).astype(F32)
    low = lse - high - mid
    row = lax.broadcasted_iota(jnp.int32, (16, width), 0)
    tail = jnp.where(row == 0, high, jnp.where(row == 1, mid, jnp.where(row == 2, low, 0.0)))
    return tail.astype(BF)


def blend(msgs, head_size):
    lses = []
    for msg in msgs:
        tail = msg[pl.ds(head_size, 16), :].astype(F32)
        lses.append(tail[0:1] + tail[1:2] + tail[2:3])
    top = functools.reduce(jnp.maximum, lses)
    total = acc = None
    for msg, lse in zip(msgs, lses):
        w = jnp.exp2(lse - top)
        part = msg[pl.ds(0, head_size), :].astype(F32) * w
        total = w if total is None else total + w
        acc = part if acc is None else acc + part
    return acc / total, top + jnp.log2(total)


def merge_kernel(head_size, n, *refs):
    out_ref = refs[-1]
    value, lse = blend([m.at[1] for m in refs[:n]], head_size)
    out_ref[pl.ds(0, head_size), :] = value.astype(BF)
    out_ref[pl.ds(head_size, 16), :] = split_lse(lse, value.shape[1])


def merge(msgs, head_size, after):
    n = len(msgs)
    vm = pl.BlockSpec(memory_space=pltpu.VMEM)
    return pl.pallas_call(
        functools.partial(merge_kernel, head_size, n),
        in_specs=[vm] * n + [pl.BlockSpec(memory_space=pl.ANY)] * len(after),
        out_specs=vm,
        out_shape=jax.ShapeDtypeStruct(msgs[0].shape[1:], BF),
        compiler_params=params(),
        name="merge",
    )(*msgs, *after)


def combine_kernel(head_size, *refs):
    msgs, (passed_ref, own_ref, own_lse_ref, out_ref) = refs[:-4], refs[-4:]
    value, lse = blend([m.at[0] for m in msgs] + [passed_ref], head_size)
    doc = value.T
    doc_lse = jnp.broadcast_to(lse, value.shape).T
    own_lse = own_lse_ref[...]
    peak = jnp.maximum(doc_lse, own_lse)
    w_doc = jnp.exp2(doc_lse - peak)
    w_own = jnp.exp2(own_lse - peak)
    out_ref[...] = ((doc * w_doc + own_ref[...] * w_own) / (w_doc + w_own)).astype(BF)


def combine(msgs, passed, own, own_lse):
    rows, head_size = own.shape
    return pl.pallas_call(
        functools.partial(combine_kernel, head_size),
        out_shape=jax.ShapeDtypeStruct((rows, head_size), BF),
        compiler_params=params(),
        name="combine",
    )(*msgs, passed, own, own_lse)


def project_kernel(z_ref, near_ref, beside_ref, *refs):
    w_refs, (out_ref, held_ref, sems) = refs[:8], refs[8:]
    copies = [
        pltpu.make_async_copy(w_refs[s], held_ref.at[s], sems.at[s]) for s in range(8)
    ]
    for copy in copies:
        copy.start()
    accs = [None, None]
    for s in range(8):
        h = lax.rem(z_ref[0] + s, 8)
        lhs = [
            jnp.concatenate(
                [
                    g_ref[:, h * 8 + j].astype(F32).reshape(-1, g_ref.shape[3]).astype(BF)
                    for j in range(8)
                ],
                1,
            )
            for g_ref in (near_ref, beside_ref)
        ]
        copies[s].wait()
        w = held_ref[s]
        for i in range(2):
            part = jnp.dot(lhs[i], w, preferred_element_type=F32)
            accs[i] = part if accs[i] is None else accs[i] + part
    for i in range(2):
        out_ref[i] = accs[i].astype(BF)


def project(z, near, beside, weights):
    chips, blocks, req, head_size = near.shape
    depth, cols = weights[0].shape
    rows = chips * req
    vm = pl.BlockSpec(memory_space=pltpu.VMEM)
    hbm = pl.BlockSpec(memory_space=pl.ANY)
    return pl.pallas_call(
        project_kernel,
        in_specs=[pl.BlockSpec(memory_space=pltpu.SMEM), vm, vm] + [hbm] * 8,
        out_specs=vm,
        out_shape=jax.ShapeDtypeStruct((2, rows, cols), BF),
        scratch_shapes=[pltpu.VMEM((8, depth, cols), BF), pltpu.SemaphoreType.DMA((8,))],
        compiler_params=params(FULL_VMEM),
        cost_estimate=pl.CostEstimate(
            flops=4 * rows * 8 * depth * cols, bytes_accessed=6 * 2**20, transcendentals=0
        ),
        name="project",
    )(z, near, beside, *weights)


def place_kernel(where_ref, *refs):
    out_ref = refs[-1]
    core, z = where_ref[0], where_ref[1]
    for s, src in enumerate(refs[:-1]):
        layer = lax.rem(z + s, 8)
        for c in range(2):
            at_core = core if c == 0 else 1 - core
            for chip in range(16):
                rep = (chip % 2) * 2 + at_core
                out_ref[chip // 2, rep, layer] = src[c, chip]


def place(where, pieces, cols):
    return pl.pallas_call(
        place_kernel,
        in_specs=[pl.BlockSpec(memory_space=pltpu.SMEM)] + [whole((2, 16, 8, cols))] * len(pieces),
        out_specs=whole((8, 4, 8, 8, cols)),
        out_shape=jax.ShapeDtypeStruct((8, 4, 8, 8, cols), BF),
        compiler_params=params(),
        name="place",
    )(where, *[p.reshape(2, 16, 8, cols) for p in pieces])


def hold_kernel(*refs):
    pass


def hold(value, until):
    hbm = pl.BlockSpec(memory_space=pl.ANY)
    return pl.pallas_call(
        hold_kernel,
        in_specs=[hbm, hbm],
        out_specs=hbm,
        out_shape=jax.ShapeDtypeStruct(value.shape, value.dtype),
        input_output_aliases={0: 0},
        compiler_params=params(),
        name="hold",
    )(value, until)


def across_x(value):
    return lax.ppermute(value, "pos", [(p, p ^ 1) for p in range(8)])


def along_y(value, dy):
    return lax.ppermute(value, "pos", [(p, (p + 2 * dy) % 8) for p in range(8)])


def head_shift(value, s):
    return lax.ppermute(value, "head", [(i, (i + s) % 8) for i in range(8)])


def other_core(value):
    return lax.ppermute(value, "rep", [(i, i ^ 1) for i in range(4)])


def body(queries, doc_keys, doc_values, suffix_keys, suffix_values, suffix_len, out_weight):
    n_req, heads, head_size = queries.shape
    keys = doc_keys.reshape(-1, head_size)
    values = doc_values.reshape(-1, head_size)
    s_keys = suffix_keys.reshape(n_req, -1, head_size)
    s_values = suffix_values.reshape(n_req, -1, head_size)
    cols = out_weight.shape[1]

    scaled = (queries.astype(F32) * (head_size ** (-0.5) * LOG2E)).astype(BF)
    ordered = scaled.reshape(8, 8, heads, head_size).transpose(0, 2, 1, 3)
    ordered = ordered.reshape(n_req * heads, head_size)
    beside = across_x(ordered)

    own, own_lse = suffix_attention(queries, s_keys, s_values, suffix_len)
    vt = transpose_values(values)
    pair = pair_up(ordered, beside, own_lse)
    arrived = {dy: along_y(pair, dy) for dy in (2, 1, 3)}
    ups, downs = [out_weight], [out_weight]

    def turn(until=None):
        if until is not None:
            ups[-1] = hold(ups[-1], until)
            if len(downs) < 4:
                downs[-1] = hold(downs[-1], until)
        ups.append(head_shift(ups[-1], 1))
        if len(downs) < 4:
            downs.append(head_shift(downs[-1], 7))

    turn()
    here = doc_attention(pair, keys, vt)
    two = doc_attention(arrived[2], keys, vt, (here, arrived[1], arrived[3]))
    two_back = along_y(two, 2)
    turn(here)
    one = doc_attention(arrived[1], keys, vt, (two,))
    one_back = along_y(one, 3)
    three = doc_attention(arrived[3], keys, vt, (one, two_back))
    three_back = along_y(three, 1)
    turn(one)
    msgs = [here, two_back, one_back, three_back]
    merged = merge(msgs, head_size, (ups[3], downs[3]))
    passed = across_x(merged)
    turn(merged)
    attended = combine(msgs, passed, own, own_lse)
    weights = [out_weight, downs[1], downs[2], downs[3], ups[4], ups[3], ups[2], ups[1]]

    rows = lax.all_to_all(attended.reshape(8, 64, head_size), "head", 0, 0, tiled=True)
    rows = hold(rows, ups[4])
    rows = rows.reshape(64, 8, head_size)
    same_core = [[chip * 2 + core for chip in range(16)] for core in range(2)]
    gathered = lax.all_to_all(
        jnp.broadcast_to(rows[None], (16,) + rows.shape),
        ("pos", "rep"),
        0,
        0,
        axis_index_groups=same_core,
        tiled=True,
    )
    beside = other_core(gathered)
    z = lax.axis_index("head").astype(jnp.int32)
    up = down = project(z[None], gathered, beside, weights)
    pieces = {0: up}
    for s in range(1, 5):
        up = head_shift(up, 1)
        pieces[8 - s] = up
        if s < 4:
            down = head_shift(down, 7)
            pieces[s] = down
    where = jnp.stack([lax.axis_index("rep").astype(jnp.int32) % 2, z])
    return place(where, [pieces[s] for s in range(8)], cols).reshape(-1, cols)


def solution(mesh):
    in_specs = (
        P(("pos", "rep"), "head", None),
        P("pos", "head", None),
        P("pos", "head", None),
        P(("pos", "rep"), None, "head", None),
        P(("pos", "rep"), None, "head", None),
        P(("pos", "rep")),
        P("head", ("pos", "rep")),
    )
    out_specs = P(None, ("pos", "rep"))
    return jax.shard_map(body, mesh=mesh, in_specs=in_specs, out_specs=out_specs, check_vma=False)
```

```python
import functools
import math

import jax
import jax.numpy as jnp
from jax import lax
from jax.experimental import pallas as pl
from jax.experimental.pallas import tpu as pltpu
from jax.sharding import PartitionSpec as P

BF = jnp.bfloat16
F32 = jnp.float32
LOG2E = math.log2(math.e)
VMEM = 32 * 2**20
SUFFIX_VMEM = 48 * 2**20
KEY_TILE = 512
MSG_ROWS = 144


def params(limit=VMEM):
    return pltpu.CompilerParams(vmem_limit_bytes=limit)


def whole(shape):
    return pl.BlockSpec(shape, lambda *_: (0,) * len(shape))


def transpose_kernel(v_ref, vt_ref):
    n_keys, head_size = v_ref.shape
    for j in range(n_keys // KEY_TILE):
        span = pl.ds(j * KEY_TILE, KEY_TILE)
        vt_ref[pl.ds(0, head_size), span] = v_ref[span, :].T
    vt_ref[pl.ds(head_size, 16), :] = jnp.ones((16, n_keys), BF)


def transpose_values(values):
    n_keys = values.shape[0]
    return pl.pallas_call(
        transpose_kernel,
        out_shape=jax.ShapeDtypeStruct((MSG_ROWS, n_keys), BF),
        compiler_params=params(),
        name="transpose_values",
    )(values)


def attend(q, k_ref, vt_ref, out_ref):
    n_keys, head_size = k_ref.shape
    tiles = n_keys // KEY_TILE

    def scores(j):
        return lax.dot_general(
            k_ref[pl.ds(pl.multiple_of(j * KEY_TILE, KEY_TILE), KEY_TILE), :],
            q,
            (((1,), (1,)), ((), ())),
            preferred_element_type=F32,
        )

    def mix(j, s, shift):
        weights = jnp.exp2(s - shift).astype(BF)
        span = pl.ds(pl.multiple_of(j * KEY_TILE, KEY_TILE), KEY_TILE)
        return jnp.dot(vt_ref[:, span], weights, preferred_element_type=F32)

    def emit(acc, shift):
        total = acc[head_size : head_size + 1]
        out_ref[pl.ds(0, head_size), :] = (acc[:head_size] / total).astype(BF)
        out_ref[pl.ds(head_size, 16), :] = split_lse(shift + jnp.log2(total), q.shape[0])

    s = scores(0)
    shift = s.max(0, keepdims=True)
    acc = None
    for j in range(tiles):
        ahead = scores(j + 1) if j + 1 < tiles else None
        part = mix(j, s, shift)
        acc = part if acc is None else acc + part
        s = ahead
    emit(acc, shift)
    worst = jnp.max(jnp.where(acc[head_size : head_size + 1] < 1e30, 0.0, 1.0))

    @pl.when(worst > 0.5)
    def _():
        top = lax.fori_loop(
            1, tiles, lambda j, top: jnp.maximum(top, scores(j).max(0, keepdims=True)), shift
        )
        again = lax.fori_loop(
            0, tiles, lambda j, total: total + mix(j, scores(j), top), jnp.zeros(acc.shape, F32)
        )
        emit(again, top)


def doc_kernel(split, q_ref, k_ref, vt_ref, *refs):
    for i in range(q_ref.shape[0]):
        attend(q_ref[i], k_ref, vt_ref, refs[i - 2] if split else refs[-1].at[i])


def doc_attention(chunks, keys, vt, after=(), split=False):
    n, rows, head_size = chunks.shape
    n_keys = keys.shape[0]
    work = n * rows * n_keys
    vm = pl.BlockSpec(memory_space=pltpu.VMEM)
    if split:
        out_shape = [jax.ShapeDtypeStruct((MSG_ROWS, rows), BF)] * n
    else:
        out_shape = jax.ShapeDtypeStruct((n, MSG_ROWS, rows), BF)
    return pl.pallas_call(
        functools.partial(doc_kernel, split),
        in_specs=[vm] * 3 + [pl.BlockSpec(memory_space=pl.ANY)] * len(after),
        out_specs=[vm] * n if split else vm,
        out_shape=out_shape,
        compiler_params=params(),
        cost_estimate=pl.CostEstimate(
            flops=10 * work * head_size, bytes_accessed=2**19, transcendentals=0
        ),
        name="doc_attention",
    )(chunks, keys, vt, *after)


def pair_kernel(a_ref, b_ref, after_ref, out_ref):
    out_ref[0] = a_ref[...]
    out_ref[1] = b_ref[...]


def pair_up(a, b, after):
    vm = pl.BlockSpec(memory_space=pltpu.VMEM)
    return pl.pallas_call(
        pair_kernel,
        in_specs=[vm, vm, pl.BlockSpec(memory_space=pl.ANY)],
        out_specs=vm,
        out_shape=jax.ShapeDtypeStruct((2,) + a.shape, a.dtype),
        compiler_params=params(),
        name="pair_up",
    )(a, b, after)


def suffix_kernel(scale, step, base, len_ref, q_ref, k_hbm, v_hbm, *refs):
    out_ref, lse_ref, k_ref, v_ref, sems = refs[-5:]
    n_req, slots, _ = k_ref.shape
    steps = n_req // step
    copies = []
    for g in range(steps):
        span = pl.ds(g * step, step)
        source = pl.ds(base + g * step, step)
        for i, (src, dst) in enumerate(((k_hbm, k_ref), (v_hbm, v_ref))):
            copies.append(pltpu.make_async_copy(src.at[source], dst.at[span], sems.at[i, g]))
            copies[-1].start()
    lane = lax.broadcasted_iota(jnp.int32, (8, slots), 1)
    for g in range(steps):
        copies[2 * g].wait()
        copies[2 * g + 1].wait()
        scored = [
            lax.dot_general(
                q_ref[base + r], k_ref[r], (((1,), (1,)), ((), ())), preferred_element_type=F32
            )
            for r in range(g * step, (g + 1) * step)
        ]
        for i in range(step):
            r = g * step + i
            live = lane < len_ref[base + r]
            s = jnp.where(live, scored[i] * scale, -1e30)
            top = s.max(1, keepdims=True)
            terms = jnp.where(live, jnp.exp2(s - top), 0.0)
            total = terms.sum(1, keepdims=True)
            mixed = jnp.dot(terms.astype(BF), v_ref[r], preferred_element_type=F32) / total
            place = pl.ds(r, 8, stride=n_req)
            out_ref[place, :] = mixed
            lse_ref[place, :] = jnp.broadcast_to(top + jnp.log2(total), mixed.shape)


def suffix_attention(queries, keys, values, lens, base, n_req, after=()):
    _, heads, head_size = queries.shape
    slots = keys.shape[1]
    step = 8
    scale = head_size ** (-0.5) * LOG2E
    wide = jax.ShapeDtypeStruct((n_req * heads, head_size), F32)
    vm = pl.BlockSpec(memory_space=pltpu.VMEM)
    hbm = pl.BlockSpec(memory_space=pl.ANY)
    return pl.pallas_call(
        functools.partial(suffix_kernel, scale, step, base),
        in_specs=[pl.BlockSpec(memory_space=pltpu.SMEM), vm, hbm, hbm] + [hbm] * len(after),
        out_specs=[vm, vm],
        out_shape=[wide, wide],
        scratch_shapes=[
            pltpu.VMEM((n_req, slots, head_size), BF),
            pltpu.VMEM((n_req, slots, head_size), BF),
            pltpu.SemaphoreType.DMA((2, n_req // step)),
        ],
        compiler_params=params(SUFFIX_VMEM),
        cost_estimate=pl.CostEstimate(
            flops=3 * 10**9, bytes_accessed=2**21, transcendentals=2**15
        ),
        name="suffix_attention",
    )(lens, queries, keys, values, *after)


def split_lse(lse, width):
    high = lse.astype(BF).astype(F32)
    mid = (lse - high).astype(BF).astype(F32)
    low = lse - high - mid
    row = lax.broadcasted_iota(jnp.int32, (16, width), 0)
    tail = jnp.where(row == 0, high, jnp.where(row == 1, mid, jnp.where(row == 2, low, 0.0)))
    return tail.astype(BF)


def blend(msgs, head_size):
    lses = []
    for msg in msgs:
        tail = msg[pl.ds(head_size, 16), :].astype(F32)
        lses.append(tail[0:1] + tail[1:2] + tail[2:3])
    top = functools.reduce(jnp.maximum, lses)
    total = acc = None
    for msg, lse in zip(msgs, lses):
        w = jnp.exp2(lse - top)
        part = msg[pl.ds(0, head_size), :].astype(F32) * w
        total = w if total is None else total + w
        acc = part if acc is None else acc + part
    return acc / total, top + jnp.log2(total)


def merge_kernel(head_size, *refs):
    out_ref = refs[-1]
    value, lse = blend([m.at[1] for m in refs[:-1]], head_size)
    out_ref[pl.ds(0, head_size), :] = value.astype(BF)
    out_ref[pl.ds(head_size, 16), :] = split_lse(lse, value.shape[1])


def merge(msgs, head_size):
    return pl.pallas_call(
        functools.partial(merge_kernel, head_size),
        out_shape=jax.ShapeDtypeStruct(msgs[0].shape[1:], BF),
        compiler_params=params(),
        name="merge",
    )(*msgs)


def combine_kernel(head_size, n_pairs, n_single, z_ref, *refs):
    pairs, rest, (keep_ref, send_ref) = refs[:n_pairs], refs[n_pairs:], refs[-2:]
    singles, own_refs = rest[:n_single], rest[n_single : n_single + 4]
    value, lse = blend([m.at[0] for m in pairs] + list(singles), head_size)
    doc = value.T
    doc_lse = jnp.broadcast_to(lse, value.shape).T
    halves = []
    for i in range(2):
        own_ref, own_lse_ref = own_refs[2 * i : 2 * i + 2]
        rows = own_ref.shape[0]
        span = slice(i * rows, (i + 1) * rows)
        own_lse = own_lse_ref[...]
        peak = jnp.maximum(doc_lse[span], own_lse)
        w_doc = jnp.exp2(doc_lse[span] - peak)
        w_own = jnp.exp2(own_lse - peak)
        halves.append((doc[span] * w_doc + own_ref[...] * w_own) / (w_doc + w_own))
    odd = lax.rem(z_ref[0], 2) == 1
    keep_ref[...] = jnp.where(odd, halves[1], halves[0]).astype(BF)
    send_ref[...] = jnp.where(odd, halves[0], halves[1]).astype(BF)


def combine(z, pairs, singles, owns, head_size, after):
    rows = pairs[0].shape[2] // 2
    vm = pl.BlockSpec(memory_space=pltpu.VMEM)
    return pl.pallas_call(
        functools.partial(combine_kernel, head_size, len(pairs), len(singles)),
        in_specs=[pl.BlockSpec(memory_space=pltpu.SMEM)]
        + [vm] * (len(pairs) + len(singles) + len(owns))
        + [pl.BlockSpec(memory_space=pl.ANY)] * len(after),
        out_specs=[vm, vm],
        out_shape=[jax.ShapeDtypeStruct((rows, head_size), BF)] * 2,
        compiler_params=params(),
        name="combine",
    )(z, *pairs, *singles, *owns, *after)


def project_kernel(z_ref, g_ref, *refs):
    near, far, outs = refs[:2], refs[2:4], refs[4:]
    groups = len(outs)
    chips = g_ref.shape[0] // groups
    blocks = g_ref.shape[1] // 2
    for s, out_ref in enumerate(outs):
        group = lax.rem(z_ref[0] // 2 + s, groups)
        at = pl.ds(group * chips, chips)
        accs = [None, None]
        for k in range(2):
            cols = [
                g_ref[at, k * blocks + j].reshape(-1, g_ref.shape[3]) for j in range(blocks)
            ]
            lhs = jnp.concatenate(cols, 1)
            for i, w_refs in enumerate((near, far)):
                part = jnp.dot(lhs, w_refs[k][...], preferred_element_type=F32)
                accs[i] = part if accs[i] is None else accs[i] + part
        for i in range(2):
            out_ref[i] = accs[i].astype(out_ref.dtype)


def project(z, gathered, near, far):
    chips, _, req, _ = gathered.shape
    cols = near[0].shape[1]
    rows = chips * req // 4
    vm = pl.BlockSpec(memory_space=pltpu.VMEM)
    return pl.pallas_call(
        project_kernel,
        in_specs=[pl.BlockSpec(memory_space=pltpu.SMEM)] + [vm] * 5,
        out_specs=[vm] * 4,
        out_shape=[
            jax.ShapeDtypeStruct((2, rows, cols), F32 if s == 0 else BF) for s in range(4)
        ],
        compiler_params=params(),
        cost_estimate=pl.CostEstimate(flops=10**9, bytes_accessed=2**22, transcendentals=0),
        name="project",
    )(z, gathered, *near, *far)


def total_kernel(own_ref, *refs):
    near_ref, far_ref = refs[-2:]
    total = own_ref[...]
    for ref in refs[:-2]:
        total = total + ref[...].astype(F32)
    near_ref[...] = total[0].astype(BF)
    far_ref[...] = total[1].astype(BF)


def add_up(parts):
    _, rows, cols = parts[0].shape
    return pl.pallas_call(
        total_kernel,
        out_shape=[jax.ShapeDtypeStruct((rows, cols), BF)] * 2,
        compiler_params=params(),
        name="add_up",
    )(*parts)


def place_kernel(where_ref, *refs):
    out_ref = refs[-1]
    core, z = where_ref[0], where_ref[1]
    for s, src in enumerate(refs[:-1]):
        layer = lax.rem(z + s, 8)
        for c in range(2):
            at_core = core if c == 0 else 1 - core
            for chip in range(4):
                pos = (layer // 2) * 2 + chip // 2
                rep = (chip % 2) * 2 + at_core
                out_ref[pos, rep, lax.rem(layer, 2)] = src[c, chip]


def place(where, pieces, cols):
    return pl.pallas_call(
        place_kernel,
        in_specs=[pl.BlockSpec(memory_space=pltpu.SMEM)] + [whole((2, 4, 32, cols))] * len(pieces),
        out_specs=whole((8, 4, 2, 32, cols)),
        out_shape=jax.ShapeDtypeStruct((8, 4, 2, 32, cols), BF),
        compiler_params=params(),
        name="place",
    )(where, *[p.reshape(2, 4, 32, cols) for p in pieces])


def across_x(value, dy=0):
    return lax.ppermute(value, "pos", [(p, ((p ^ 1) + 2 * dy) % 8) for p in range(8)])


def along_y(value, dy):
    return lax.ppermute(value, "pos", [(p, (p + 2 * dy) % 8) for p in range(8)])


def head_shift(value, s):
    return lax.ppermute(value, "head", [(i, (i + s) % 8) for i in range(8)])


def head_twin(value):
    return lax.ppermute(value, "head", [(i, i ^ 1) for i in range(8)])


def other_core(value):
    return lax.ppermute(value, "rep", [(i, i ^ 1) for i in range(4)])


def body(queries, doc_keys, doc_values, suffix_keys, suffix_values, suffix_len, out_weight):
    n_req, heads, head_size = queries.shape
    keys = doc_keys.reshape(-1, head_size)
    values = doc_values.reshape(-1, head_size)
    s_keys = suffix_keys.reshape(n_req, -1, head_size)
    s_values = suffix_values.reshape(n_req, -1, head_size)
    cols = out_weight.shape[1]

    scaled = (queries.astype(F32) * (head_size ** (-0.5) * LOG2E)).astype(BF)
    ordered = scaled.reshape(2, n_req // 2, heads, head_size).transpose(0, 2, 1, 3)
    ordered = ordered.reshape(n_req * heads, head_size)
    beside = across_x(ordered)

    half = n_req // 2
    suffix = (queries, s_keys, s_values, suffix_len)
    early = suffix_attention(*suffix, 0, half)
    vt = transpose_values(values)
    pair = pair_up(ordered, beside, early[1])
    arrived = {dy: along_y(pair, dy) for dy in (2, 1, 3)}
    far = [other_core(out_weight)]
    near = [out_weight, head_twin(out_weight)]
    far.append(head_twin(far[0]))

    here = doc_attention(pair, keys, vt)
    two = doc_attention(arrived[2], keys, vt, (here, arrived[1], arrived[3], far[0]))
    two_back = along_y(two, 2)
    one = doc_attention(arrived[1], keys, vt, (two,))
    one_back = along_y(one, 3)
    three = doc_attention(arrived[3], keys, vt, (one, near[1]), split=True)
    three_back = along_y(three[0], 1)
    three_across = across_x(three[1], 1)
    passed = across_x(merge([here, two_back, one_back], head_size))
    late = suffix_attention(*suffix, half, half, (three[0],))
    z = lax.axis_index("head").astype(jnp.int32)
    keep, send = combine(
        z[None],
        [here, two_back, one_back],
        [three_back, three_across, passed],
        early + late,
        head_size,
        (far[1],),
    )

    rows = jnp.stack([keep, head_twin(send)]).reshape(2 * heads, half, head_size)
    same_core = [[chip * 2 + core for chip in range(16)] for core in range(2)]
    gathered = lax.all_to_all(
        jnp.broadcast_to(rows[None], (16,) + rows.shape),
        ("pos", "rep"),
        0,
        0,
        axis_index_groups=same_core,
        tiled=True,
    )
    parts = project(z[None], gathered, near, far)
    mine, other = add_up([parts[0]] + [head_shift(parts[s], 2 * s) for s in (2, 1, 3)])
    up = down = jnp.stack([mine, other_core(other)])
    pieces = {0: up}
    for s in range(1, 5):
        up = head_shift(up, 1)
        pieces[8 - s] = up
        if s < 4:
            down = head_shift(down, 7)
            pieces[s] = down
    where = jnp.stack([lax.axis_index("rep").astype(jnp.int32) % 2, z])
    return place(where, [pieces[s] for s in range(8)], cols).reshape(-1, cols)


def solution(mesh):
    in_specs = (
        P(("pos", "rep"), "head", None),
        P("pos", "head", None),
        P("pos", "head", None),
        P(("pos", "rep"), None, "head", None),
        P(("pos", "rep"), None, "head", None),
        P(("pos", "rep")),
        P("head", ("pos", "rep")),
    )
    out_specs = P(None, ("pos", "rep"))
    return jax.shard_map(body, mesh=mesh, in_specs=in_specs, out_specs=out_specs, check_vma=False)
```

```python
import functools
import math

import jax
import jax.numpy as jnp
from jax import lax
from jax.experimental import pallas as pl
from jax.experimental.pallas import tpu as pltpu
from jax.sharding import PartitionSpec as P

BF = jnp.bfloat16
F32 = jnp.float32
LOG2E = math.log2(math.e)
VMEM = 32 * 2**20
SUFFIX_VMEM = 48 * 2**20
KEY_TILE = 512
MSG_ROWS = 144


def params(limit=VMEM):
    return pltpu.CompilerParams(vmem_limit_bytes=limit)


def whole(shape):
    return pl.BlockSpec(shape, lambda *_: (0,) * len(shape))


def transpose_kernel(v_ref, vt_ref):
    n_keys, head_size = v_ref.shape
    for j in range(n_keys // KEY_TILE):
        span = pl.ds(j * KEY_TILE, KEY_TILE)
        vt_ref[pl.ds(0, head_size), span] = v_ref[span, :].T
    vt_ref[pl.ds(head_size, 16), :] = jnp.ones((16, n_keys), BF)


def transpose_values(values):
    n_keys = values.shape[0]
    return pl.pallas_call(
        transpose_kernel,
        out_shape=jax.ShapeDtypeStruct((MSG_ROWS, n_keys), BF),
        compiler_params=params(),
        name="transpose_values",
    )(values)


def attend(q, k_ref, vt_ref, out_ref):
    n_keys, head_size = k_ref.shape
    tiles = n_keys // KEY_TILE

    def scores(j):
        return lax.dot_general(
            k_ref[pl.ds(pl.multiple_of(j * KEY_TILE, KEY_TILE), KEY_TILE), :],
            q,
            (((1,), (1,)), ((), ())),
            preferred_element_type=F32,
        )

    def mix(j, s, shift):
        weights = jnp.exp2(s - shift).astype(BF)
        span = pl.ds(pl.multiple_of(j * KEY_TILE, KEY_TILE), KEY_TILE)
        return jnp.dot(vt_ref[:, span], weights, preferred_element_type=F32)

    def emit(acc, shift):
        total = acc[head_size : head_size + 1]
        out_ref[pl.ds(0, head_size), :] = (acc[:head_size] / total).astype(BF)
        out_ref[pl.ds(head_size, 16), :] = split_lse(shift + jnp.log2(total), q.shape[0])

    s = scores(0)
    shift = s.max(0, keepdims=True)
    acc = None
    for j in range(tiles):
        ahead = scores(j + 1) if j + 1 < tiles else None
        part = mix(j, s, shift)
        acc = part if acc is None else acc + part
        s = ahead
    emit(acc, shift)
    worst = jnp.max(jnp.where(acc[head_size : head_size + 1] < 1e30, 0.0, 1.0))

    @pl.when(worst > 0.5)
    def _():
        top = lax.fori_loop(
            1, tiles, lambda j, top: jnp.maximum(top, scores(j).max(0, keepdims=True)), shift
        )
        again = lax.fori_loop(
            0, tiles, lambda j, total: total + mix(j, scores(j), top), jnp.zeros(acc.shape, F32)
        )
        emit(again, top)


def doc_kernel(split, q_ref, k_ref, vt_ref, *refs):
    for i in range(q_ref.shape[0]):
        attend(q_ref[i], k_ref, vt_ref, refs[i - 2] if split else refs[-1].at[i])


def doc_attention(chunks, keys, vt, after=(), split=False):
    n, rows, head_size = chunks.shape
    n_keys = keys.shape[0]
    work = n * rows * n_keys
    vm = pl.BlockSpec(memory_space=pltpu.VMEM)
    if split:
        out_shape = [jax.ShapeDtypeStruct((MSG_ROWS, rows), BF)] * n
    else:
        out_shape = jax.ShapeDtypeStruct((n, MSG_ROWS, rows), BF)
    return pl.pallas_call(
        functools.partial(doc_kernel, split),
        in_specs=[vm] * 3 + [pl.BlockSpec(memory_space=pl.ANY)] * len(after),
        out_specs=[vm] * n if split else vm,
        out_shape=out_shape,
        compiler_params=params(),
        cost_estimate=pl.CostEstimate(
            flops=10 * work * head_size, bytes_accessed=2**19, transcendentals=0
        ),
        name="doc_attention",
    )(chunks, keys, vt, *after)


def suffix_kernel(scale, step, base, len_ref, q_ref, k_hbm, v_hbm, *refs):
    out_ref, lse_ref, k_ref, v_ref, sems = refs[-5:]
    n_req, slots, _ = k_ref.shape
    steps = n_req // step
    copies = []
    for g in range(steps):
        span = pl.ds(g * step, step)
        source = pl.ds(base + g * step, step)
        for i, (src, dst) in enumerate(((k_hbm, k_ref), (v_hbm, v_ref))):
            copies.append(pltpu.make_async_copy(src.at[source], dst.at[span], sems.at[i, g]))
            copies[-1].start()
    lane = lax.broadcasted_iota(jnp.int32, (8, slots), 1)
    for g in range(steps):
        copies[2 * g].wait()
        copies[2 * g + 1].wait()
        scored = [
            lax.dot_general(
                q_ref[base + r], k_ref[r], (((1,), (1,)), ((), ())), preferred_element_type=F32
            )
            for r in range(g * step, (g + 1) * step)
        ]
        for i in range(step):
            r = g * step + i
            live = lane < len_ref[base + r]
            s = jnp.where(live, scored[i] * scale, -1e30)
            top = s.max(1, keepdims=True)
            terms = jnp.where(live, jnp.exp2(s - top), 0.0)
            total = terms.sum(1, keepdims=True)
            mixed = jnp.dot(terms.astype(BF), v_ref[r], preferred_element_type=F32) / total
            place = pl.ds(r, 8, stride=n_req)
            out_ref[place, :] = mixed
            lse_ref[place, :] = jnp.broadcast_to(top + jnp.log2(total), mixed.shape)


def suffix_attention(queries, keys, values, lens, base, n_req, after=()):
    _, heads, head_size = queries.shape
    slots = keys.shape[1]
    step = 8
    scale = head_size ** (-0.5) * LOG2E
    wide = jax.ShapeDtypeStruct((n_req * heads, head_size), F32)
    vm = pl.BlockSpec(memory_space=pltpu.VMEM)
    hbm = pl.BlockSpec(memory_space=pl.ANY)
    return pl.pallas_call(
        functools.partial(suffix_kernel, scale, step, base),
        in_specs=[pl.BlockSpec(memory_space=pltpu.SMEM), vm, hbm, hbm] + [hbm] * len(after),
        out_specs=[vm, vm],
        out_shape=[wide, wide],
        scratch_shapes=[
            pltpu.VMEM((n_req, slots, head_size), BF),
            pltpu.VMEM((n_req, slots, head_size), BF),
            pltpu.SemaphoreType.DMA((2, n_req // step)),
        ],
        compiler_params=params(SUFFIX_VMEM),
        cost_estimate=pl.CostEstimate(
            flops=3 * 10**9, bytes_accessed=2**21, transcendentals=2**15
        ),
        name="suffix_attention",
    )(lens, queries, keys, values, *after)


def split_lse(lse, width):
    high = lse.astype(BF).astype(F32)
    mid = (lse - high).astype(BF).astype(F32)
    low = lse - high - mid
    row = lax.broadcasted_iota(jnp.int32, (16, width), 0)
    tail = jnp.where(row == 0, high, jnp.where(row == 1, mid, jnp.where(row == 2, low, 0.0)))
    return tail.astype(BF)


def blend(msgs, head_size):
    lses = []
    for msg in msgs:
        tail = msg[pl.ds(head_size, 16), :].astype(F32)
        lses.append(tail[0:1] + tail[1:2] + tail[2:3])
    top = functools.reduce(jnp.maximum, lses)
    total = acc = None
    for msg, lse in zip(msgs, lses):
        w = jnp.exp2(lse - top)
        part = msg[pl.ds(0, head_size), :].astype(F32) * w
        total = w if total is None else total + w
        acc = part if acc is None else acc + part
    return acc / total, top + jnp.log2(total)


def merge_kernel(head_size, *refs):
    out_ref = refs[-1]
    value, lse = blend([m.at[1] for m in refs[:-1]], head_size)
    out_ref[pl.ds(0, head_size), :] = value.astype(BF)
    out_ref[pl.ds(head_size, 16), :] = split_lse(lse, value.shape[1])


def merge(msgs, head_size):
    return pl.pallas_call(
        functools.partial(merge_kernel, head_size),
        out_shape=jax.ShapeDtypeStruct(msgs[0].shape[1:], BF),
        compiler_params=params(),
        name="merge",
    )(*msgs)


def combine_kernel(head_size, n_pairs, n_single, z_ref, *refs):
    pairs, rest, (keep_ref, send_ref) = refs[:n_pairs], refs[n_pairs:], refs[-2:]
    singles, own_refs = rest[:n_single], rest[n_single : n_single + 4]
    value, lse = blend([m.at[0] for m in pairs] + list(singles), head_size)
    doc = value.T
    doc_lse = jnp.broadcast_to(lse, value.shape).T
    halves = []
    for i in range(2):
        own_ref, own_lse_ref = own_refs[2 * i : 2 * i + 2]
        rows = own_ref.shape[0]
        span = slice(i * rows, (i + 1) * rows)
        own_lse = own_lse_ref[...]
        peak = jnp.maximum(doc_lse[span], own_lse)
        w_doc = jnp.exp2(doc_lse[span] - peak)
        w_own = jnp.exp2(own_lse - peak)
        halves.append((doc[span] * w_doc + own_ref[...] * w_own) / (w_doc + w_own))
    odd = lax.rem(z_ref[0], 2) == 1
    keep_ref[...] = jnp.where(odd, halves[1], halves[0]).astype(BF)
    send_ref[...] = jnp.where(odd, halves[0], halves[1]).astype(BF)


def combine(z, pairs, singles, owns, head_size, after):
    rows = pairs[0].shape[2] // 2
    vm = pl.BlockSpec(memory_space=pltpu.VMEM)
    return pl.pallas_call(
        functools.partial(combine_kernel, head_size, len(pairs), len(singles)),
        in_specs=[pl.BlockSpec(memory_space=pltpu.SMEM)]
        + [vm] * (len(pairs) + len(singles) + len(owns))
        + [pl.BlockSpec(memory_space=pl.ANY)] * len(after),
        out_specs=[vm, vm],
        out_shape=[jax.ShapeDtypeStruct((rows, head_size), BF)] * 2,
        compiler_params=params(),
        name="combine",
    )(z, *pairs, *singles, *owns, *after)


def project_kernel(where_ref, *refs):
    pieces, near, far, outs, held_ref = refs[:4], refs[4:6], refs[6:8], refs[8:12], refs[12]
    core, z, y, x = where_ref[0], where_ref[1], where_ref[2], where_ref[3]
    for second, g_ref in enumerate(pieces):
        blocks = g_ref.shape[1] // 2
        accs = [None, None]
        for k in range(2):
            cols = [g_ref[:, k * blocks + j].reshape(-1, g_ref.shape[3]) for j in range(blocks)]
            lhs = jnp.concatenate(cols, 1)
            for i, w_refs in enumerate((near, far)):
                part = jnp.dot(lhs, w_refs[k][...], preferred_element_type=F32)
                accs[i] = part if accs[i] is None else accs[i] + part
        req = g_ref.shape[2]
        for first in range(4):
            dy = jnp.where(core == 0, first, second)
            dx = jnp.where(core == 0, second, first)
            group = lax.rem(y + 4 - dy, 4)
            chip = lax.rem(x + 4 - dx, 4)
            to = lax.rem(group + 4 - z // 2, 4)
            for i in range(2):
                held_ref[to, i, chip] = accs[i][first * req : (first + 1) * req]
    for s, out_ref in enumerate(outs):
        out_ref[...] = held_ref[s].astype(out_ref.dtype)


def project(where, pieces, near, far):
    _, _, req, _ = pieces[0].shape
    cols = near[0].shape[1]
    vm = pl.BlockSpec(memory_space=pltpu.VMEM)
    return pl.pallas_call(
        project_kernel,
        in_specs=[pl.BlockSpec(memory_space=pltpu.SMEM)] + [vm] * 8,
        out_specs=[vm] * 4,
        out_shape=[
            jax.ShapeDtypeStruct((2, 4, req, cols), F32 if s == 0 else BF) for s in range(4)
        ],
        scratch_shapes=[pltpu.VMEM((4, 2, 4, req, cols), F32)],
        compiler_params=params(),
        cost_estimate=pl.CostEstimate(flops=10**9, bytes_accessed=2**22, transcendentals=0),
        name="project",
    )(where, *pieces, *near, *far)


def total_kernel(own_ref, *refs):
    near_ref, far_ref = refs[-2:]
    total = own_ref[...]
    for ref in refs[:-2]:
        total = total + ref[...].astype(F32)
    near_ref[...] = total[0].astype(BF)
    far_ref[...] = total[1].astype(BF)


def add_up(parts):
    _, chips, req, cols = parts[0].shape
    return pl.pallas_call(
        total_kernel,
        out_shape=[jax.ShapeDtypeStruct((chips, req, cols), BF)] * 2,
        compiler_params=params(),
        name="add_up",
    )(*parts)


def place_kernel(where_ref, *refs):
    out_ref = refs[-1]
    core, z = where_ref[0], where_ref[1]
    for s, src in enumerate(refs[:-1]):
        layer = lax.rem(z + s, 8)
        for c in range(2):
            at_core = core if c == 0 else 1 - core
            for chip in range(4):
                pos = (layer // 2) * 2 + chip % 2
                rep = (chip // 2) * 2 + at_core
                out_ref[pos, rep, lax.rem(layer, 2)] = src[c, chip]


def place(where, pieces, cols):
    return pl.pallas_call(
        place_kernel,
        in_specs=[pl.BlockSpec(memory_space=pltpu.SMEM)] + [whole((2, 4, 32, cols))] * len(pieces),
        out_specs=whole((8, 4, 2, 32, cols)),
        out_shape=jax.ShapeDtypeStruct((8, 4, 2, 32, cols), BF),
        compiler_params=params(),
        name="place",
    )(where, *pieces)


def across_x(value, dy=0):
    return lax.ppermute(value, "pos", [(p, ((p ^ 1) + 2 * dy) % 8) for p in range(8)])


def along_y(value, dy):
    return lax.ppermute(value, "pos", [(p, (p + 2 * dy) % 8) for p in range(8)])


def across_plane(value, s, first):
    pairs = []
    for pos in range(8):
        for rep in range(4):
            y, x, core = pos // 2, (rep // 2) * 2 + pos % 2, rep % 2
            if (core == 0) == first:
                y = (y + s) % 4
            else:
                x = (x + s) % 4
            pairs.append((pos * 4 + rep, (y * 2 + x % 2) * 4 + (x // 2) * 2 + core))
    return lax.ppermute(value, ("pos", "rep"), pairs)


def head_shift(value, s):
    return lax.ppermute(value, "head", [(i, (i + s) % 8) for i in range(8)])


def head_twin(value):
    return lax.ppermute(value, "head", [(i, i ^ 1) for i in range(8)])


def other_core(value):
    return lax.ppermute(value, "rep", [(i, i ^ 1) for i in range(4)])


def body(queries, doc_keys, doc_values, suffix_keys, suffix_values, suffix_len, out_weight):
    n_req, heads, head_size = queries.shape
    keys = doc_keys.reshape(-1, head_size)
    values = doc_values.reshape(-1, head_size)
    s_keys = suffix_keys.reshape(n_req, -1, head_size)
    s_values = suffix_values.reshape(n_req, -1, head_size)
    cols = out_weight.shape[1]

    scaled = (queries.astype(F32) * (head_size ** (-0.5) * LOG2E)).astype(BF)
    ordered = scaled.reshape(2, n_req // 2, heads, head_size).transpose(0, 2, 1, 3)
    ordered = ordered.reshape(n_req * heads, head_size)
    beside = across_x(ordered)

    half = n_req // 2
    suffix = (queries, s_keys, s_values, suffix_len)
    vt = transpose_values(values)
    pair = jnp.stack([ordered, beside])
    arrived = {dy: along_y(pair, dy) for dy in (2, 1, 3)}
    far = [other_core(out_weight)]
    near = [out_weight, head_twin(out_weight)]
    far.append(head_twin(far[0]))

    here = doc_attention(pair, keys, vt)
    early = suffix_attention(*suffix, 0, half, (here,))
    two = doc_attention(arrived[2], keys, vt, (here, arrived[1], arrived[3], far[0], early[1]))
    two_back = along_y(two, 2)
    one = doc_attention(arrived[1], keys, vt, (two,))
    one_back = along_y(one, 3)
    three = doc_attention(arrived[3], keys, vt, (one, near[1]), split=True)
    three_back = along_y(three[0], 1)
    three_across = across_x(three[1], 1)
    passed = across_x(merge([here, two_back, one_back], head_size))
    late = suffix_attention(*suffix, half, half, (three[0],))
    z = lax.axis_index("head").astype(jnp.int32)
    keep, send = combine(
        z[None],
        [here, two_back, one_back],
        [three_back, three_across, passed],
        early + late,
        head_size,
        (far[1],),
    )

    rows = jnp.stack([keep, head_twin(send)]).reshape(2 * heads, half, head_size)
    first = [rows] + [across_plane(rows, s, True) for s in (1, 2, 3)]
    first = jnp.stack(first)
    second = [first] + [across_plane(first, s, False) for s in (1, 2, 3)]
    pos, rep = lax.axis_index("pos"), lax.axis_index("rep")
    where = jnp.stack([rep % 2, z, pos // 2, (rep // 2) * 2 + pos % 2]).astype(jnp.int32)
    parts = project(where, second, near, far)
    mine, other = add_up([parts[0]] + [head_shift(parts[s], 2 * s) for s in (2, 1, 3)])
    up = down = jnp.stack([mine, other_core(other)])
    pieces = {0: up}
    for s in range(1, 5):
        up = head_shift(up, 1)
        pieces[8 - s] = up
        if s < 4:
            down = head_shift(down, 7)
            pieces[s] = down
    return place(where, [pieces[s] for s in range(8)], cols).reshape(-1, cols)


def solution(mesh):
    in_specs = (
        P(("pos", "rep"), "head", None),
        P("pos", "head", None),
        P("pos", "head", None),
        P(("pos", "rep"), None, "head", None),
        P(("pos", "rep"), None, "head", None),
        P(("pos", "rep")),
        P("head", ("pos", "rep")),
    )
    out_specs = P(None, ("pos", "rep"))
    return jax.shard_map(body, mesh=mesh, in_specs=in_specs, out_specs=out_specs, check_vma=False)
```

```python
import functools
import math

import jax
import jax.numpy as jnp
from jax import lax
from jax.experimental import pallas as pl
from jax.experimental.pallas import tpu as pltpu
from jax.sharding import PartitionSpec as P

BF = jnp.bfloat16
F32 = jnp.float32
LOG2E = math.log2(math.e)
VMEM = 32 * 2**20
SUFFIX_VMEM = 48 * 2**20
KEY_TILE = 512
MSG_ROWS = 144


def params(limit=VMEM):
    return pltpu.CompilerParams(vmem_limit_bytes=limit)


def whole(shape):
    return pl.BlockSpec(shape, lambda *_: (0,) * len(shape))


def transpose_kernel(v_ref, vt_ref):
    n_keys, head_size = v_ref.shape
    for j in range(n_keys // KEY_TILE):
        span = pl.ds(j * KEY_TILE, KEY_TILE)
        vt_ref[pl.ds(0, head_size), span] = v_ref[span, :].T
    vt_ref[pl.ds(head_size, 16), :] = jnp.ones((16, n_keys), BF)


def transpose_values(values):
    n_keys = values.shape[0]
    return pl.pallas_call(
        transpose_kernel,
        out_shape=jax.ShapeDtypeStruct((MSG_ROWS, n_keys), BF),
        compiler_params=params(),
        name="transpose_values",
    )(values)


def attend(q, k_ref, vt_ref, out_ref):
    n_keys, head_size = k_ref.shape
    tiles = n_keys // KEY_TILE

    def scores(j):
        return lax.dot_general(
            k_ref[pl.ds(pl.multiple_of(j * KEY_TILE, KEY_TILE), KEY_TILE), :],
            q,
            (((1,), (1,)), ((), ())),
            preferred_element_type=F32,
        )

    def mix(j, s, shift):
        weights = jnp.exp2(s - shift).astype(BF)
        span = pl.ds(pl.multiple_of(j * KEY_TILE, KEY_TILE), KEY_TILE)
        return jnp.dot(vt_ref[:, span], weights, preferred_element_type=F32)

    def emit(acc, shift):
        total = acc[head_size : head_size + 1]
        out_ref[pl.ds(0, head_size), :] = (acc[:head_size] / total).astype(BF)
        out_ref[pl.ds(head_size, 16), :] = split_lse(shift + jnp.log2(total), q.shape[0])

    s = scores(0)
    shift = s.max(0, keepdims=True)
    acc = None
    for j in range(tiles):
        ahead = scores(j + 1) if j + 1 < tiles else None
        part = mix(j, s, shift)
        acc = part if acc is None else acc + part
        s = ahead
    emit(acc, shift)
    worst = jnp.max(jnp.where(acc[head_size : head_size + 1] < 1e30, 0.0, 1.0))

    @pl.when(worst > 0.5)
    def _():
        top = lax.fori_loop(
            1, tiles, lambda j, top: jnp.maximum(top, scores(j).max(0, keepdims=True)), shift
        )
        again = lax.fori_loop(
            0, tiles, lambda j, total: total + mix(j, scores(j), top), jnp.zeros(acc.shape, F32)
        )
        emit(again, top)


def doc_kernel(split, q_ref, k_ref, vt_ref, *refs):
    for i in range(q_ref.shape[0]):
        attend(q_ref[i], k_ref, vt_ref, refs[i - 2] if split else refs[-1].at[i])


def doc_attention(chunks, keys, vt, after=(), split=False):
    n, rows, head_size = chunks.shape
    n_keys = keys.shape[0]
    work = n * rows * n_keys
    vm = pl.BlockSpec(memory_space=pltpu.VMEM)
    if split:
        out_shape = [jax.ShapeDtypeStruct((MSG_ROWS, rows), BF)] * n
    else:
        out_shape = jax.ShapeDtypeStruct((n, MSG_ROWS, rows), BF)
    return pl.pallas_call(
        functools.partial(doc_kernel, split),
        in_specs=[vm] * 3 + [pl.BlockSpec(memory_space=pl.ANY)] * len(after),
        out_specs=[vm] * n if split else vm,
        out_shape=out_shape,
        compiler_params=params(),
        cost_estimate=pl.CostEstimate(
            flops=10 * work * head_size, bytes_accessed=2**19, transcendentals=0
        ),
        name="doc_attention",
    )(chunks, keys, vt, *after)


def suffix_kernel(scale, step, base, len_ref, q_ref, k_hbm, v_hbm, *refs):
    out_ref, lse_ref, k_ref, v_ref, sems = refs[-5:]
    n_req, slots, _ = k_ref.shape
    steps = n_req // step
    copies = []
    for g in range(steps):
        span = pl.ds(g * step, step)
        source = pl.ds(base + g * step, step)
        for i, (src, dst) in enumerate(((k_hbm, k_ref), (v_hbm, v_ref))):
            copies.append(pltpu.make_async_copy(src.at[source], dst.at[span], sems.at[i, g]))
            copies[-1].start()
    lane = lax.broadcasted_iota(jnp.int32, (8, slots), 1)
    for g in range(steps):
        copies[2 * g].wait()
        copies[2 * g + 1].wait()
        scored = [
            lax.dot_general(
                q_ref[base + r], k_ref[r], (((1,), (1,)), ((), ())), preferred_element_type=F32
            )
            for r in range(g * step, (g + 1) * step)
        ]
        for i in range(step):
            r = g * step + i
            live = lane < len_ref[base + r]
            s = jnp.where(live, scored[i] * scale, -1e30)
            top = s.max(1, keepdims=True)
            terms = jnp.where(live, jnp.exp2(s - top), 0.0)
            total = terms.sum(1, keepdims=True)
            mixed = jnp.dot(terms.astype(BF), v_ref[r], preferred_element_type=F32) / total
            place = pl.ds(r, 8, stride=n_req)
            out_ref[place, :] = mixed
            lse_ref[place, :] = jnp.broadcast_to(top + jnp.log2(total), mixed.shape)


def suffix_attention(queries, keys, values, lens, base, n_req, after=()):
    _, heads, head_size = queries.shape
    slots = keys.shape[1]
    step = 8
    scale = head_size ** (-0.5) * LOG2E
    wide = jax.ShapeDtypeStruct((n_req * heads, head_size), F32)
    vm = pl.BlockSpec(memory_space=pltpu.VMEM)
    hbm = pl.BlockSpec(memory_space=pl.ANY)
    return pl.pallas_call(
        functools.partial(suffix_kernel, scale, step, base),
        in_specs=[pl.BlockSpec(memory_space=pltpu.SMEM), vm, hbm, hbm] + [hbm] * len(after),
        out_specs=[vm, vm],
        out_shape=[wide, wide],
        scratch_shapes=[
            pltpu.VMEM((n_req, slots, head_size), BF),
            pltpu.VMEM((n_req, slots, head_size), BF),
            pltpu.SemaphoreType.DMA((2, n_req // step)),
        ],
        compiler_params=params(SUFFIX_VMEM),
        cost_estimate=pl.CostEstimate(
            flops=3 * 10**9, bytes_accessed=2**21, transcendentals=2**15
        ),
        name="suffix_attention",
    )(lens, queries, keys, values, *after)


def split_lse(lse, width):
    high = lse.astype(BF).astype(F32)
    mid = (lse - high).astype(BF).astype(F32)
    low = lse - high - mid
    row = lax.broadcasted_iota(jnp.int32, (16, width), 0)
    tail = jnp.where(row == 0, high, jnp.where(row == 1, mid, jnp.where(row == 2, low, 0.0)))
    return tail.astype(BF)


def blend(msgs, head_size):
    lses = []
    for msg in msgs:
        tail = msg[pl.ds(head_size, 16), :].astype(F32)
        lses.append(tail[0:1] + tail[1:2] + tail[2:3])
    top = functools.reduce(jnp.maximum, lses)
    total = acc = None
    for msg, lse in zip(msgs, lses):
        w = jnp.exp2(lse - top)
        part = msg[pl.ds(0, head_size), :].astype(F32) * w
        total = w if total is None else total + w
        acc = part if acc is None else acc + part
    return acc / total, top + jnp.log2(total)


def merge_kernel(head_size, *refs):
    out_ref = refs[-1]
    value, lse = blend([m.at[1] for m in refs[:-1]], head_size)
    out_ref[pl.ds(0, head_size), :] = value.astype(BF)
    out_ref[pl.ds(head_size, 16), :] = split_lse(lse, value.shape[1])


def merge(msgs, head_size):
    return pl.pallas_call(
        functools.partial(merge_kernel, head_size),
        out_shape=jax.ShapeDtypeStruct(msgs[0].shape[1:], BF),
        compiler_params=params(),
        name="merge",
    )(*msgs)


def combine_kernel(head_size, n_pairs, n_single, z_ref, *refs):
    pairs, rest, (keep_ref, send_ref) = refs[:n_pairs], refs[n_pairs:], refs[-2:]
    singles, own_refs = rest[:n_single], rest[n_single : n_single + 4]
    value, lse = blend([m.at[0] for m in pairs] + list(singles), head_size)
    doc = value.T
    doc_lse = jnp.broadcast_to(lse, value.shape).T
    halves = []
    for i in range(2):
        own_ref, own_lse_ref = own_refs[2 * i : 2 * i + 2]
        rows = own_ref.shape[0]
        span = slice(i * rows, (i + 1) * rows)
        own_lse = own_lse_ref[...]
        peak = jnp.maximum(doc_lse[span], own_lse)
        w_doc = jnp.exp2(doc_lse[span] - peak)
        w_own = jnp.exp2(own_lse - peak)
        halves.append((doc[span] * w_doc + own_ref[...] * w_own) / (w_doc + w_own))
    odd = lax.rem(z_ref[0], 2) == 1
    keep_ref[...] = jnp.where(odd, halves[1], halves[0]).astype(BF)
    send_ref[...] = jnp.where(odd, halves[0], halves[1]).astype(BF)


def combine(z, pairs, singles, owns, head_size, after):
    rows = pairs[0].shape[2] // 2
    vm = pl.BlockSpec(memory_space=pltpu.VMEM)
    return pl.pallas_call(
        functools.partial(combine_kernel, head_size, len(pairs), len(singles)),
        in_specs=[pl.BlockSpec(memory_space=pltpu.SMEM)]
        + [vm] * (len(pairs) + len(singles) + len(owns))
        + [pl.BlockSpec(memory_space=pl.ANY)] * len(after),
        out_specs=[vm, vm],
        out_shape=[jax.ShapeDtypeStruct((rows, head_size), BF)] * 2,
        compiler_params=params(),
        name="combine",
    )(z, *pairs, *singles, *owns, *after)


def project_kernel(n, seconds, where_ref, *refs):
    pieces, near, far, rest = refs[:n], refs[n : n + 2], refs[n + 2 : n + 4], refs[n + 4 :]
    core, z, y, x = where_ref[0], where_ref[1], where_ref[2], where_ref[3]
    held_ref = rest[0]
    if len(rest) > 1:
        held_ref = rest[-1]
        held_ref[...] = rest[0][...]
    blocks = pieces[0].shape[1] // 2
    req, head_size = pieces[0].shape[2:]
    at = 0
    for second, n_first in seconds:
        group_refs = []
        while sum(g.shape[0] for g in group_refs) < n_first:
            group_refs.append(pieces[at])
            at += 1
        accs = [None, None]
        for k in range(2):
            cols = []
            for j in range(blocks):
                parts = [g[:, k * blocks + j].reshape(-1, head_size) for g in group_refs]
                cols.append(jnp.concatenate(parts, 0) if len(parts) > 1 else parts[0])
            lhs = jnp.concatenate(cols, 1)
            for i, w_refs in enumerate((near, far)):
                part = jnp.dot(lhs, w_refs[k][...], preferred_element_type=F32)
                accs[i] = part if accs[i] is None else accs[i] + part
        for first in range(4):
            dy = jnp.where(core == 0, first, second)
            dx = jnp.where(core == 0, second, first)
            group = lax.rem(y + 4 - dy, 4)
            chip = lax.rem(x + 4 - dx, 4)
            to = lax.rem(group + 4 - z // 2, 4)
            for i in range(2):
                held_ref[to, i, chip] = accs[i][first * req : (first + 1) * req].astype(BF)
    if len(rest) > 1:
        for s, out_ref in enumerate(rest[1:-1]):
            out_ref[...] = held_ref[s]


def project(where, pieces, seconds, near, far, so_far=None):
    req = pieces[0].shape[2]
    cols = near[0].shape[1]
    part = (2, 4, req, cols)
    vm = pl.BlockSpec(memory_space=pltpu.VMEM)
    extra = [] if so_far is None else [so_far]
    whole_share = jax.ShapeDtypeStruct((4,) + part, BF)
    return pl.pallas_call(
        functools.partial(project_kernel, len(pieces), seconds),
        in_specs=[pl.BlockSpec(memory_space=pltpu.SMEM)] + [vm] * (len(pieces) + 4 + len(extra)),
        out_specs=[vm] * 4 if extra else vm,
        out_shape=[jax.ShapeDtypeStruct(part, BF)] * 4 if extra else whole_share,
        scratch_shapes=[pltpu.VMEM(whole_share.shape, BF)] if extra else [],
        compiler_params=params(),
        cost_estimate=pl.CostEstimate(flops=2 * 10**9, bytes_accessed=2**22, transcendentals=0),
        name="project",
    )(where, *pieces, *near, *far, *extra)


def total_kernel(own_ref, *refs):
    near_ref, far_ref = refs[-2:]
    total = own_ref[...]
    for ref in refs[:-2]:
        total = total + ref[...].astype(F32)
    near_ref[...] = total[0].astype(BF)
    far_ref[...] = total[1].astype(BF)


def add_up(parts):
    _, chips, req, cols = parts[0].shape
    return pl.pallas_call(
        total_kernel,
        out_shape=[jax.ShapeDtypeStruct((chips, req, cols), BF)] * 2,
        compiler_params=params(),
        name="add_up",
    )(*parts)


def place_kernel(where_ref, *refs):
    out_ref = refs[-1]
    core, z = where_ref[0], where_ref[1]
    for s, src in enumerate(refs[:-1]):
        layer = lax.rem(z + s, 8)
        for c in range(2):
            at_core = core if c == 0 else 1 - core
            for chip in range(4):
                pos = (layer // 2) * 2 + chip % 2
                rep = (chip // 2) * 2 + at_core
                out_ref[pos, rep, lax.rem(layer, 2)] = src[c, chip]


def place(where, pieces, cols):
    return pl.pallas_call(
        place_kernel,
        in_specs=[pl.BlockSpec(memory_space=pltpu.SMEM)] + [whole((2, 4, 32, cols))] * len(pieces),
        out_specs=whole((8, 4, 2, 32, cols)),
        out_shape=jax.ShapeDtypeStruct((8, 4, 2, 32, cols), BF),
        compiler_params=params(),
        name="place",
    )(where, *pieces)


def across_x(value, dy=0):
    return lax.ppermute(value, "pos", [(p, ((p ^ 1) + 2 * dy) % 8) for p in range(8)])


def along_y(value, dy):
    return lax.ppermute(value, "pos", [(p, (p + 2 * dy) % 8) for p in range(8)])


def across_plane(value, s, first):
    pairs = []
    for pos in range(8):
        for rep in range(4):
            y, x, core = pos // 2, (rep // 2) * 2 + pos % 2, rep % 2
            if (core == 0) == first:
                y = (y + s) % 4
            else:
                x = (x + s) % 4
            pairs.append((pos * 4 + rep, (y * 2 + x % 2) * 4 + (x // 2) * 2 + core))
    return lax.ppermute(value, ("pos", "rep"), pairs)


def head_shift(value, s):
    return lax.ppermute(value, "head", [(i, (i + s) % 8) for i in range(8)])


def head_twin(value):
    return lax.ppermute(value, "head", [(i, i ^ 1) for i in range(8)])


def other_core(value):
    return lax.ppermute(value, "rep", [(i, i ^ 1) for i in range(4)])


def body(queries, doc_keys, doc_values, suffix_keys, suffix_values, suffix_len, out_weight):
    n_req, heads, head_size = queries.shape
    keys = doc_keys.reshape(-1, head_size)
    values = doc_values.reshape(-1, head_size)
    s_keys = suffix_keys.reshape(n_req, -1, head_size)
    s_values = suffix_values.reshape(n_req, -1, head_size)
    cols = out_weight.shape[1]

    scaled = (queries.astype(F32) * (head_size ** (-0.5) * LOG2E)).astype(BF)
    ordered = scaled.reshape(2, n_req // 2, heads, head_size).transpose(0, 2, 1, 3)
    ordered = ordered.reshape(n_req * heads, head_size)
    beside = across_x(ordered)

    half = n_req // 2
    suffix = (queries, s_keys, s_values, suffix_len)
    vt = transpose_values(values)
    pair = jnp.stack([ordered, beside])
    arrived = {dy: along_y(pair, dy) for dy in (2, 1, 3)}
    far = [other_core(out_weight)]
    near = [out_weight, head_twin(out_weight)]
    far.append(head_twin(far[0]))

    here = doc_attention(pair, keys, vt)
    early = suffix_attention(*suffix, 0, half, (here,))
    two = doc_attention(arrived[2], keys, vt, (here, arrived[1], arrived[3], far[0], early[1]))
    two_back = along_y(two, 2)
    one = doc_attention(arrived[1], keys, vt, (two,))
    one_back = along_y(one, 3)
    three = doc_attention(arrived[3], keys, vt, (one, near[1]), split=True)
    three_back = along_y(three[0], 1)
    three_across = across_x(three[1], 1)
    passed = across_x(merge([here, two_back, one_back], head_size))
    late = suffix_attention(*suffix, half, half, (three[0],))
    z = lax.axis_index("head").astype(jnp.int32)
    keep, send = combine(
        z[None],
        [here, two_back, one_back],
        [three_back, three_across, passed],
        early + late,
        head_size,
        (far[1],),
    )

    rows = jnp.stack([keep, head_twin(send)]).reshape(2 * heads, half, head_size)
    low = jnp.stack([rows, across_plane(rows, 1, True)])
    below_low = across_plane(low, 1, False)
    high = jnp.stack([across_plane(rows, s, True) for s in (2, 3)])
    above_high = across_plane(high, 3, False)
    above_low, below_high = across_plane(low, 3, False), across_plane(high, 1, False)
    opposite = [across_plane(below_low, 1, False), across_plane(above_high, 3, False)]
    pos, rep = lax.axis_index("pos"), lax.axis_index("rep")
    where = jnp.stack([rep % 2, z, pos // 2, (rep // 2) * 2 + pos % 2]).astype(jnp.int32)
    ready = [low, high, below_low, below_high, above_low, above_high]
    share = project(where, ready, ((0, 4), (1, 4), (3, 4)), near, far)
    parts = project(where, opposite, ((2, 4),), near, far, share)
    mine, other = add_up([parts[0]] + [head_shift(parts[s], 2 * s) for s in (2, 1, 3)])
    up = down = jnp.stack([mine, other_core(other)])
    pieces = {0: up}
    for s in range(1, 5):
        up = head_shift(up, 1)
        pieces[8 - s] = up
        if s < 4:
            down = head_shift(down, 7)
            pieces[s] = down
    return place(where, [pieces[s] for s in range(8)], cols).reshape(-1, cols)


def solution(mesh):
    in_specs = (
        P(("pos", "rep"), "head", None),
        P("pos", "head", None),
        P("pos", "head", None),
        P(("pos", "rep"), None, "head", None),
        P(("pos", "rep"), None, "head", None),
        P(("pos", "rep")),
        P("head", ("pos", "rep")),
    )
    out_specs = P(None, ("pos", "rep"))
    return jax.shard_map(body, mesh=mesh, in_specs=in_specs, out_specs=out_specs, check_vma=False)
```

```python
import functools
import math

import jax
import jax.numpy as jnp
from jax import lax
from jax.experimental import pallas as pl
from jax.experimental.pallas import tpu as pltpu
from jax.sharding import PartitionSpec as P

BF = jnp.bfloat16
F32 = jnp.float32
LOG2E = math.log2(math.e)
VMEM = 32 * 2**20
SUFFIX_VMEM = 48 * 2**20
KEY_TILE = 512
MSG_ROWS = 144


def params(limit=VMEM):
    return pltpu.CompilerParams(vmem_limit_bytes=limit)


def whole(shape):
    return pl.BlockSpec(shape, lambda *_: (0,) * len(shape))


def transpose_kernel(v_ref, vt_ref):
    n_keys, head_size = v_ref.shape
    for j in range(n_keys // KEY_TILE):
        span = pl.ds(j * KEY_TILE, KEY_TILE)
        vt_ref[pl.ds(0, head_size), span] = v_ref[span, :].T
    vt_ref[pl.ds(head_size, 16), :] = jnp.ones((16, n_keys), BF)


def transpose_values(values):
    n_keys = values.shape[0]
    return pl.pallas_call(
        transpose_kernel,
        out_shape=jax.ShapeDtypeStruct((MSG_ROWS, n_keys), BF),
        compiler_params=params(),
        name="transpose_values",
    )(values)


def attend(q, k_ref, vt_ref, out_ref):
    n_keys, head_size = k_ref.shape
    tiles = n_keys // KEY_TILE

    def scores(j):
        return lax.dot_general(
            k_ref[pl.ds(pl.multiple_of(j * KEY_TILE, KEY_TILE), KEY_TILE), :],
            q,
            (((1,), (1,)), ((), ())),
            preferred_element_type=F32,
        )

    def mix(j, s, shift):
        weights = jnp.exp2(s - shift).astype(BF)
        span = pl.ds(pl.multiple_of(j * KEY_TILE, KEY_TILE), KEY_TILE)
        return jnp.dot(vt_ref[:, span], weights, preferred_element_type=F32)

    def emit(acc, shift):
        total = acc[head_size : head_size + 1]
        out_ref[pl.ds(0, head_size), :] = (acc[:head_size] / total).astype(BF)
        out_ref[pl.ds(head_size, 16), :] = split_lse(shift + jnp.log2(total), q.shape[0])

    s = scores(0)
    shift = s.max(0, keepdims=True)
    acc = None
    for j in range(tiles):
        ahead = scores(j + 1) if j + 1 < tiles else None
        part = mix(j, s, shift)
        acc = part if acc is None else acc + part
        s = ahead
    emit(acc, shift)
    worst = jnp.max(jnp.where(acc[head_size : head_size + 1] < 1e30, 0.0, 1.0))

    @pl.when(worst > 0.5)
    def _():
        top = lax.fori_loop(
            1, tiles, lambda j, top: jnp.maximum(top, scores(j).max(0, keepdims=True)), shift
        )
        again = lax.fori_loop(
            0, tiles, lambda j, total: total + mix(j, scores(j), top), jnp.zeros(acc.shape, F32)
        )
        emit(again, top)


def doc_kernel(split, q_ref, k_ref, vt_ref, *refs):
    for i in range(q_ref.shape[0]):
        attend(q_ref[i], k_ref, vt_ref, refs[i - 2] if split else refs[-1].at[i])


def doc_attention(chunks, keys, vt, after=(), split=False):
    n, rows, head_size = chunks.shape
    n_keys = keys.shape[0]
    work = n * rows * n_keys
    vm = pl.BlockSpec(memory_space=pltpu.VMEM)
    if split:
        out_shape = [jax.ShapeDtypeStruct((MSG_ROWS, rows), BF)] * n
    else:
        out_shape = jax.ShapeDtypeStruct((n, MSG_ROWS, rows), BF)
    return pl.pallas_call(
        functools.partial(doc_kernel, split),
        in_specs=[vm] * 3 + [pl.BlockSpec(memory_space=pl.ANY)] * len(after),
        out_specs=[vm] * n if split else vm,
        out_shape=out_shape,
        compiler_params=params(),
        cost_estimate=pl.CostEstimate(
            flops=10 * work * head_size, bytes_accessed=2**19, transcendentals=0
        ),
        name="doc_attention",
    )(chunks, keys, vt, *after)


def pair_kernel(scale, a_ref, b_ref, out_ref, held_ref):
    n_req, heads, head_size = a_ref.shape
    half = n_req // 2
    for i, ref in enumerate((a_ref, b_ref)):
        held_ref[...] = (ref[...].astype(F32) * scale).reshape(held_ref.shape)
        for parity in range(2):
            for h in range(heads):
                base = parity * half * heads
                block = held_ref[pl.ds(base + h, half, stride=heads), :]
                out_ref[i, pl.ds(base + h * half, half), :] = block.astype(BF)


def pair_up(a, b):
    n_req, heads, head_size = a.shape
    rows = n_req * heads
    return pl.pallas_call(
        functools.partial(pair_kernel, head_size ** (-0.5) * LOG2E),
        out_shape=jax.ShapeDtypeStruct((2, rows, head_size), BF),
        scratch_shapes=[pltpu.VMEM((rows, head_size), F32)],
        compiler_params=params(),
        name="pair_up",
    )(a, b)


def suffix_kernel(scale, step, base, len_ref, q_ref, k_hbm, v_hbm, *refs):
    out_ref, lse_ref, k_ref, v_ref, sems = refs[-5:]
    n_req, slots, _ = k_ref.shape
    steps = n_req // step
    copies = []
    for g in range(steps):
        span = pl.ds(g * step, step)
        source = pl.ds(base + g * step, step)
        for i, (src, dst) in enumerate(((k_hbm, k_ref), (v_hbm, v_ref))):
            copies.append(pltpu.make_async_copy(src.at[source], dst.at[span], sems.at[i, g]))
            copies[-1].start()
    lane = lax.broadcasted_iota(jnp.int32, (8, slots), 1)
    for g in range(steps):
        copies[2 * g].wait()
        copies[2 * g + 1].wait()
        scored = [
            lax.dot_general(
                q_ref[base + r], k_ref[r], (((1,), (1,)), ((), ())), preferred_element_type=F32
            )
            for r in range(g * step, (g + 1) * step)
        ]
        for i in range(step):
            r = g * step + i
            live = lane < len_ref[base + r]
            s = jnp.where(live, scored[i] * scale, -1e30)
            top = s.max(1, keepdims=True)
            terms = jnp.where(live, jnp.exp2(s - top), 0.0)
            total = terms.sum(1, keepdims=True)
            mixed = jnp.dot(terms.astype(BF), v_ref[r], preferred_element_type=F32) / total
            place = pl.ds(r, 8, stride=n_req)
            out_ref[place, :] = mixed
            lse_ref[place, :] = jnp.broadcast_to(top + jnp.log2(total), mixed.shape)


def suffix_attention(queries, keys, values, lens, base, n_req, after=()):
    _, heads, head_size = queries.shape
    slots = keys.shape[1]
    step = 8
    scale = head_size ** (-0.5) * LOG2E
    wide = jax.ShapeDtypeStruct((n_req * heads, head_size), F32)
    vm = pl.BlockSpec(memory_space=pltpu.VMEM)
    hbm = pl.BlockSpec(memory_space=pl.ANY)
    return pl.pallas_call(
        functools.partial(suffix_kernel, scale, step, base),
        in_specs=[pl.BlockSpec(memory_space=pltpu.SMEM), vm, hbm, hbm] + [hbm] * len(after),
        out_specs=[vm, vm],
        out_shape=[wide, wide],
        scratch_shapes=[
            pltpu.VMEM((n_req, slots, head_size), BF),
            pltpu.VMEM((n_req, slots, head_size), BF),
            pltpu.SemaphoreType.DMA((2, n_req // step)),
        ],
        compiler_params=params(SUFFIX_VMEM),
        cost_estimate=pl.CostEstimate(
            flops=3 * 10**9, bytes_accessed=2**21, transcendentals=2**15
        ),
        name="suffix_attention",
    )(lens, queries, keys, values, *after)


def split_lse(lse, width):
    high = lse.astype(BF).astype(F32)
    mid = (lse - high).astype(BF).astype(F32)
    low = lse - high - mid
    row = lax.broadcasted_iota(jnp.int32, (16, width), 0)
    tail = jnp.where(row == 0, high, jnp.where(row == 1, mid, jnp.where(row == 2, low, 0.0)))
    return tail.astype(BF)


def blend(msgs, head_size):
    lses = []
    for msg in msgs:
        tail = msg[pl.ds(head_size, 16), :].astype(F32)
        lses.append(tail[0:1] + tail[1:2] + tail[2:3])
    top = functools.reduce(jnp.maximum, lses)
    total = acc = None
    for msg, lse in zip(msgs, lses):
        w = jnp.exp2(lse - top)
        part = msg[pl.ds(0, head_size), :].astype(F32) * w
        total = w if total is None else total + w
        acc = part if acc is None else acc + part
    return acc / total, top + jnp.log2(total)


def merge_kernel(head_size, *refs):
    out_ref = refs[-1]
    value, lse = blend([m.at[1] for m in refs[:-1]], head_size)
    out_ref[pl.ds(0, head_size), :] = value.astype(BF)
    out_ref[pl.ds(head_size, 16), :] = split_lse(lse, value.shape[1])


def merge(msgs, head_size):
    return pl.pallas_call(
        functools.partial(merge_kernel, head_size),
        out_shape=jax.ShapeDtypeStruct(msgs[0].shape[1:], BF),
        compiler_params=params(),
        name="merge",
    )(*msgs)


def combine_kernel(head_size, n_pairs, n_single, z_ref, *refs):
    pairs, rest, (keep_ref, send_ref) = refs[:n_pairs], refs[n_pairs:], refs[-2:]
    singles, own_refs = rest[:n_single], rest[n_single : n_single + 4]
    value, lse = blend([m.at[0] for m in pairs] + list(singles), head_size)
    doc = value.T
    doc_lse = jnp.broadcast_to(lse, value.shape).T
    halves = []
    for i in range(2):
        own_ref, own_lse_ref = own_refs[2 * i : 2 * i + 2]
        rows = own_ref.shape[0]
        span = slice(i * rows, (i + 1) * rows)
        own_lse = own_lse_ref[...]
        peak = jnp.maximum(doc_lse[span], own_lse)
        w_doc = jnp.exp2(doc_lse[span] - peak)
        w_own = jnp.exp2(own_lse - peak)
        halves.append((doc[span] * w_doc + own_ref[...] * w_own) / (w_doc + w_own))
    odd = lax.rem(z_ref[0], 2) == 1
    keep_ref[...] = jnp.where(odd, halves[1], halves[0]).astype(BF)
    send_ref[...] = jnp.where(odd, halves[0], halves[1]).astype(BF)


def combine(z, pairs, singles, owns, head_size, after):
    rows = pairs[0].shape[2] // 2
    vm = pl.BlockSpec(memory_space=pltpu.VMEM)
    return pl.pallas_call(
        functools.partial(combine_kernel, head_size, len(pairs), len(singles)),
        in_specs=[pl.BlockSpec(memory_space=pltpu.SMEM)]
        + [vm] * (len(pairs) + len(singles) + len(owns))
        + [pl.BlockSpec(memory_space=pl.ANY)] * len(after),
        out_specs=[vm, vm],
        out_shape=[jax.ShapeDtypeStruct((rows, head_size), BF)] * 2,
        compiler_params=params(),
        name="combine",
    )(z, *pairs, *singles, *owns, *after)


def project_kernel(n, seconds, where_ref, *refs):
    pieces, near, far, rest = refs[:n], refs[n : n + 2], refs[n + 2 : n + 4], refs[n + 4 :]
    core, z, y, x = where_ref[0], where_ref[1], where_ref[2], where_ref[3]
    held_ref = rest[0]
    if len(rest) > 1:
        held_ref = rest[-1]
        held_ref[...] = rest[0][...]
    blocks = pieces[0].shape[1] // 2
    req, head_size = pieces[0].shape[2:]
    at = 0
    for second, n_first in seconds:
        group_refs = []
        while sum(g.shape[0] for g in group_refs) < n_first:
            group_refs.append(pieces[at])
            at += 1
        accs = [None, None]
        for k in range(2):
            cols = []
            for j in range(blocks):
                parts = [g[:, k * blocks + j].reshape(-1, head_size) for g in group_refs]
                cols.append(jnp.concatenate(parts, 0) if len(parts) > 1 else parts[0])
            lhs = jnp.concatenate(cols, 1)
            for i, w_refs in enumerate((near, far)):
                part = jnp.dot(lhs, w_refs[k][...], preferred_element_type=F32)
                accs[i] = part if accs[i] is None else accs[i] + part
        for first in range(4):
            dy = jnp.where(core == 0, first, second)
            dx = jnp.where(core == 0, second, first)
            group = lax.rem(y + 4 - dy, 4)
            chip = lax.rem(x + 4 - dx, 4)
            to = lax.rem(group + 4 - z // 2, 4)
            for i in range(2):
                held_ref[to, i, chip] = accs[i][first * req : (first + 1) * req].astype(BF)
    if len(rest) > 1:
        for s, out_ref in enumerate(rest[1:-1]):
            out_ref[...] = held_ref[s]


def project(where, pieces, seconds, near, far, so_far=None):
    req = pieces[0].shape[2]
    cols = near[0].shape[1]
    part = (2, 4, req, cols)
    vm = pl.BlockSpec(memory_space=pltpu.VMEM)
    extra = [] if so_far is None else [so_far]
    whole_share = jax.ShapeDtypeStruct((4,) + part, BF)
    return pl.pallas_call(
        functools.partial(project_kernel, len(pieces), seconds),
        in_specs=[pl.BlockSpec(memory_space=pltpu.SMEM)] + [vm] * (len(pieces) + 4 + len(extra)),
        out_specs=[vm] * 4 if extra else vm,
        out_shape=[jax.ShapeDtypeStruct(part, BF)] * 4 if extra else whole_share,
        scratch_shapes=[pltpu.VMEM(whole_share.shape, BF)] if extra else [],
        compiler_params=params(),
        cost_estimate=pl.CostEstimate(flops=2 * 10**9, bytes_accessed=2**22, transcendentals=0),
        name="project",
    )(where, *pieces, *near, *far, *extra)


def total_kernel(own_ref, *refs):
    near_ref, far_ref = refs[-2:]
    total = own_ref[...]
    for ref in refs[:-2]:
        total = total + ref[...].astype(F32)
    near_ref[...] = total[0].astype(BF)
    far_ref[...] = total[1].astype(BF)


def add_up(parts):
    _, chips, req, cols = parts[0].shape
    return pl.pallas_call(
        total_kernel,
        out_shape=[jax.ShapeDtypeStruct((chips, req, cols), BF)] * 2,
        compiler_params=params(),
        name="add_up",
    )(*parts)


def slabs(where_ref, s, n_slabs):
    core, z = where_ref[0], where_ref[1]
    layer = lax.rem(z + s, 8)
    found = []
    for c in range(2):
        at_core = core if c == 0 else 1 - core
        for chip in range(n_slabs):
            pos = (layer // 2) * 2 + chip % 2
            rep = (chip // 2) * 2 + at_core
            found.append(((c, chip), (pos, rep, lax.rem(layer, 2))))
    return found


def place_kernel(steps, where_ref, *refs):
    out_ref = refs[-1]
    for s, src in zip(steps, refs[:-1]):
        for of, to in slabs(where_ref, s, src.shape[1]):
            out_ref[to] = src[of]


def place(where, pieces, steps, cols):
    return pl.pallas_call(
        functools.partial(place_kernel, steps),
        in_specs=[pl.BlockSpec(memory_space=pltpu.SMEM)] + [whole(p.shape) for p in pieces],
        out_specs=whole((8, 4, 2, 32, cols)),
        out_shape=jax.ShapeDtypeStruct((8, 4, 2, 32, cols), BF),
        compiler_params=params(),
        name="place",
    )(where, *pieces)


def place_last_kernel(step, where_ref, src_ref, _, out_ref, sems):
    copies = [
        pltpu.make_async_copy(src_ref.at[of], out_ref.at[to], sems.at[i])
        for i, (of, to) in enumerate(slabs(where_ref, step, src_ref.shape[1]))
    ]
    for copy in copies:
        copy.start()
    for copy in copies:
        copy.wait()


def place_last(where, piece, step, placed):
    hbm = pl.BlockSpec(memory_space=pl.ANY)
    return pl.pallas_call(
        functools.partial(place_last_kernel, step),
        in_specs=[
            pl.BlockSpec(memory_space=pltpu.SMEM),
            pl.BlockSpec(memory_space=pltpu.VMEM),
            hbm,
        ],
        out_specs=hbm,
        out_shape=jax.ShapeDtypeStruct(placed.shape, BF),
        scratch_shapes=[pltpu.SemaphoreType.DMA((8,))],
        input_output_aliases={2: 0},
        compiler_params=params(),
        name="place_last",
    )(where, piece, placed)


def across_x(value, dy=0):
    return lax.ppermute(value, "pos", [(p, ((p ^ 1) + 2 * dy) % 8) for p in range(8)])


def along_y(value, dy):
    return lax.ppermute(value, "pos", [(p, (p + 2 * dy) % 8) for p in range(8)])


def across_plane(value, s, first):
    pairs = []
    for pos in range(8):
        for rep in range(4):
            y, x, core = pos // 2, (rep // 2) * 2 + pos % 2, rep % 2
            if (core == 0) == first:
                y = (y + s) % 4
            else:
                x = (x + s) % 4
            pairs.append((pos * 4 + rep, (y * 2 + x % 2) * 4 + (x // 2) * 2 + core))
    return lax.ppermute(value, ("pos", "rep"), pairs)


def head_shift(value, s):
    return lax.ppermute(value, "head", [(i, (i + s) % 8) for i in range(8)])


def head_twin(value):
    return lax.ppermute(value, "head", [(i, i ^ 1) for i in range(8)])


def other_core(value):
    return lax.ppermute(value, "rep", [(i, i ^ 1) for i in range(4)])


def body(queries, doc_keys, doc_values, suffix_keys, suffix_values, suffix_len, out_weight):
    n_req, heads, head_size = queries.shape
    keys = doc_keys.reshape(-1, head_size)
    values = doc_values.reshape(-1, head_size)
    s_keys = suffix_keys.reshape(n_req, -1, head_size)
    s_values = suffix_values.reshape(n_req, -1, head_size)
    cols = out_weight.shape[1]

    beside = across_x(queries)

    half = n_req // 2
    suffix = (queries, s_keys, s_values, suffix_len)
    vt = transpose_values(values)
    pair = pair_up(queries, beside)
    arrived = {dy: along_y(pair, dy) for dy in (2, 1, 3)}
    far = [other_core(out_weight)]
    near = [out_weight, head_twin(out_weight)]
    far.append(head_twin(far[0]))

    here = doc_attention(pair, keys, vt)
    early = suffix_attention(*suffix, 0, half, (here,))
    two = doc_attention(arrived[2], keys, vt, (here, arrived[1], arrived[3], far[0], early[1]))
    two_back = along_y(two, 2)
    one = doc_attention(arrived[1], keys, vt, (two,))
    one_back = along_y(one, 3)
    three = doc_attention(arrived[3], keys, vt, (one, near[1]), split=True)
    three_back = along_y(three[0], 1)
    three_across = across_x(three[1], 1)
    passed = across_x(merge([here, two_back, one_back], head_size))
    late = suffix_attention(*suffix, half, half, (three[0],))
    z = lax.axis_index("head").astype(jnp.int32)
    keep, send = combine(
        z[None],
        [here, two_back, one_back],
        [three_back, three_across, passed],
        early + late,
        head_size,
        (far[1],),
    )

    rows = jnp.stack([keep, head_twin(send)]).reshape(2 * heads, half, head_size)
    low = jnp.stack([rows, across_plane(rows, 1, True)])
    below_low = across_plane(low, 1, False)
    high = jnp.stack([across_plane(rows, s, True) for s in (2, 3)])
    above_high = across_plane(high, 3, False)
    above_low, below_high = across_plane(low, 3, False), across_plane(high, 1, False)
    opposite = [across_plane(below_low, 1, False), across_plane(above_high, 3, False)]
    pos, rep = lax.axis_index("pos"), lax.axis_index("rep")
    where = jnp.stack([rep % 2, z, pos // 2, (rep // 2) * 2 + pos % 2]).astype(jnp.int32)
    ready = [low, high, below_low, below_high, above_low, above_high]
    share = project(where, ready, ((0, 4), (1, 4), (3, 4)), near, far)
    parts = project(where, opposite, ((2, 4),), near, far, share)
    mine, other = add_up([parts[0]] + [head_shift(parts[s], 2 * s) for s in (2, 1, 3)])
    up = down = jnp.stack([mine, other_core(other)])
    pieces = {0: up}
    for s in range(1, 5):
        up = head_shift(up, 1)
        pieces[8 - s] = up
        if s < 4:
            down = head_shift(down, 7)
            pieces[s] = down
    steps = (0, 1, 2, 3, 5, 6, 7)
    placed = place(where, [pieces[s] for s in steps], steps, cols)
    return place_last(where, pieces[4], 4, placed).reshape(-1, cols)


def solution(mesh):
    in_specs = (
        P(("pos", "rep"), "head", None),
        P("pos", "head", None),
        P("pos", "head", None),
        P(("pos", "rep"), None, "head", None),
        P(("pos", "rep"), None, "head", None),
        P(("pos", "rep")),
        P("head", ("pos", "rep")),
    )
    out_specs = P(None, ("pos", "rep"))
    return jax.shard_map(body, mesh=mesh, in_specs=in_specs, out_specs=out_specs, check_vma=False)
```

```python
import functools
import math

import jax
import jax.numpy as jnp
from jax import lax
from jax.experimental import pallas as pl
from jax.experimental.pallas import tpu as pltpu
from jax.sharding import PartitionSpec as P

BF = jnp.bfloat16
F32 = jnp.float32
LOG2E = math.log2(math.e)
VMEM = 32 * 2**20
SUFFIX_VMEM = 48 * 2**20
KEY_TILE = 512
MSG_ROWS = 144


def params(limit=VMEM):
    return pltpu.CompilerParams(vmem_limit_bytes=limit)


def whole(shape):
    return pl.BlockSpec(shape, lambda *_: (0,) * len(shape))


def transpose_kernel(v_ref, vt_ref):
    n_keys, head_size = v_ref.shape
    for j in range(n_keys // KEY_TILE):
        span = pl.ds(j * KEY_TILE, KEY_TILE)
        vt_ref[pl.ds(0, head_size), span] = v_ref[span, :].T
    vt_ref[pl.ds(head_size, 16), :] = jnp.ones((16, n_keys), BF)


def transpose_values(values):
    n_keys = values.shape[0]
    return pl.pallas_call(
        transpose_kernel,
        out_shape=jax.ShapeDtypeStruct((MSG_ROWS, n_keys), BF),
        compiler_params=params(),
        name="transpose_values",
    )(values)


def attend(q, k_ref, vt_ref, out_ref):
    n_keys, head_size = k_ref.shape
    tiles = n_keys // KEY_TILE

    def scores(j):
        return lax.dot_general(
            k_ref[pl.ds(pl.multiple_of(j * KEY_TILE, KEY_TILE), KEY_TILE), :],
            q,
            (((1,), (1,)), ((), ())),
            preferred_element_type=F32,
        )

    def mix(j, s, shift):
        weights = jnp.exp2(s - shift).astype(BF)
        span = pl.ds(pl.multiple_of(j * KEY_TILE, KEY_TILE), KEY_TILE)
        return jnp.dot(vt_ref[:, span], weights, preferred_element_type=F32)

    def emit(acc, shift):
        total = acc[head_size : head_size + 1]
        out_ref[pl.ds(0, head_size), :] = (acc[:head_size] / total).astype(BF)
        out_ref[pl.ds(head_size, 16), :] = split_lse(shift + jnp.log2(total), q.shape[0])

    s = scores(0)
    shift = s.max(0, keepdims=True)
    acc = None
    for j in range(tiles):
        ahead = scores(j + 1) if j + 1 < tiles else None
        part = mix(j, s, shift)
        acc = part if acc is None else acc + part
        s = ahead
    emit(acc, shift)
    worst = jnp.max(jnp.where(acc[head_size : head_size + 1] < 1e30, 0.0, 1.0))

    @pl.when(worst > 0.5)
    def _():
        top = lax.fori_loop(
            1, tiles, lambda j, top: jnp.maximum(top, scores(j).max(0, keepdims=True)), shift
        )
        again = lax.fori_loop(
            0, tiles, lambda j, total: total + mix(j, scores(j), top), jnp.zeros(acc.shape, F32)
        )
        emit(again, top)


def doc_kernel(split, q_ref, k_ref, vt_ref, *refs):
    for i in range(q_ref.shape[0]):
        attend(q_ref[i], k_ref, vt_ref, refs[i - 2] if split else refs[-1].at[i])


def doc_attention(chunks, keys, vt, after=(), split=False):
    n, rows, head_size = chunks.shape
    n_keys = keys.shape[0]
    work = n * rows * n_keys
    vm = pl.BlockSpec(memory_space=pltpu.VMEM)
    if split:
        out_shape = [jax.ShapeDtypeStruct((MSG_ROWS, rows), BF)] * n
    else:
        out_shape = jax.ShapeDtypeStruct((n, MSG_ROWS, rows), BF)
    return pl.pallas_call(
        functools.partial(doc_kernel, split),
        in_specs=[vm] * 3 + [pl.BlockSpec(memory_space=pl.ANY)] * len(after),
        out_specs=[vm] * n if split else vm,
        out_shape=out_shape,
        compiler_params=params(),
        cost_estimate=pl.CostEstimate(
            flops=10 * work * head_size, bytes_accessed=2**19, transcendentals=0
        ),
        name="doc_attention",
    )(chunks, keys, vt, *after)


def pair_kernel(scale, a_ref, b_ref, out_ref, held_ref):
    n_req, heads, head_size = a_ref.shape
    half = n_req // 2
    for i, ref in enumerate((a_ref, b_ref)):
        held_ref[...] = (ref[...].astype(F32) * scale).reshape(held_ref.shape)
        for parity in range(2):
            for h in range(heads):
                base = parity * half * heads
                block = held_ref[pl.ds(base + h, half, stride=heads), :]
                out_ref[i, pl.ds(base + h * half, half), :] = block.astype(BF)


def pair_up(a, b):
    n_req, heads, head_size = a.shape
    rows = n_req * heads
    return pl.pallas_call(
        functools.partial(pair_kernel, head_size ** (-0.5) * LOG2E),
        out_shape=jax.ShapeDtypeStruct((2, rows, head_size), BF),
        scratch_shapes=[pltpu.VMEM((rows, head_size), F32)],
        compiler_params=params(),
        name="pair_up",
    )(a, b)


def suffix_kernel(scale, step, base, len_ref, q_ref, k_hbm, v_hbm, *refs):
    out_ref, lse_ref, k_ref, v_ref, sems = refs[-5:]
    n_req, slots, _ = k_ref.shape
    steps = n_req // step
    copies = []
    for g in range(steps):
        span = pl.ds(g * step, step)
        source = pl.ds(base + g * step, step)
        for i, (src, dst) in enumerate(((k_hbm, k_ref), (v_hbm, v_ref))):
            copies.append(pltpu.make_async_copy(src.at[source], dst.at[span], sems.at[i, g]))
            copies[-1].start()
    lane = lax.broadcasted_iota(jnp.int32, (8, slots), 1)
    for g in range(steps):
        copies[2 * g].wait()
        copies[2 * g + 1].wait()
        scored = [
            lax.dot_general(
                q_ref[base + r], k_ref[r], (((1,), (1,)), ((), ())), preferred_element_type=F32
            )
            for r in range(g * step, (g + 1) * step)
        ]
        for i in range(step):
            r = g * step + i
            live = lane < len_ref[base + r]
            s = jnp.where(live, scored[i] * scale, -1e30)
            top = s.max(1, keepdims=True)
            terms = jnp.where(live, jnp.exp2(s - top), 0.0)
            total = terms.sum(1, keepdims=True)
            mixed = jnp.dot(terms.astype(BF), v_ref[r], preferred_element_type=F32) / total
            place = pl.ds(r, 8, stride=n_req)
            out_ref[place, :] = mixed
            lse_ref[place, :] = jnp.broadcast_to(top + jnp.log2(total), mixed.shape)


def suffix_attention(queries, keys, values, lens, base, n_req, after=()):
    _, heads, head_size = queries.shape
    slots = keys.shape[1]
    step = 8
    scale = head_size ** (-0.5) * LOG2E
    wide = jax.ShapeDtypeStruct((n_req * heads, head_size), F32)
    vm = pl.BlockSpec(memory_space=pltpu.VMEM)
    hbm = pl.BlockSpec(memory_space=pl.ANY)
    return pl.pallas_call(
        functools.partial(suffix_kernel, scale, step, base),
        in_specs=[pl.BlockSpec(memory_space=pltpu.SMEM), vm, hbm, hbm] + [hbm] * len(after),
        out_specs=[vm, vm],
        out_shape=[wide, wide],
        scratch_shapes=[
            pltpu.VMEM((n_req, slots, head_size), BF),
            pltpu.VMEM((n_req, slots, head_size), BF),
            pltpu.SemaphoreType.DMA((2, n_req // step)),
        ],
        compiler_params=params(SUFFIX_VMEM),
        cost_estimate=pl.CostEstimate(
            flops=3 * 10**9, bytes_accessed=2**21, transcendentals=2**15
        ),
        name="suffix_attention",
    )(lens, queries, keys, values, *after)


def split_lse(lse, width):
    high = lse.astype(BF).astype(F32)
    mid = (lse - high).astype(BF).astype(F32)
    low = lse - high - mid
    row = lax.broadcasted_iota(jnp.int32, (16, width), 0)
    tail = jnp.where(row == 0, high, jnp.where(row == 1, mid, jnp.where(row == 2, low, 0.0)))
    return tail.astype(BF)


def blend(msgs, head_size):
    lses = []
    for msg in msgs:
        tail = msg[pl.ds(head_size, 16), :].astype(F32)
        lses.append(tail[0:1] + tail[1:2] + tail[2:3])
    top = functools.reduce(jnp.maximum, lses)
    total = acc = None
    for msg, lse in zip(msgs, lses):
        w = jnp.exp2(lse - top)
        part = msg[pl.ds(0, head_size), :].astype(F32) * w
        total = w if total is None else total + w
        acc = part if acc is None else acc + part
    return acc / total, top + jnp.log2(total)


def merge_kernel(head_size, *refs):
    out_ref = refs[-1]
    value, lse = blend([m.at[1] for m in refs[:-1]], head_size)
    out_ref[pl.ds(0, head_size), :] = value.astype(BF)
    out_ref[pl.ds(head_size, 16), :] = split_lse(lse, value.shape[1])


def merge(msgs, head_size):
    return pl.pallas_call(
        functools.partial(merge_kernel, head_size),
        out_shape=jax.ShapeDtypeStruct(msgs[0].shape[1:], BF),
        compiler_params=params(),
        name="merge",
    )(*msgs)


def combine_kernel(head_size, n_pairs, n_single, z_ref, *refs):
    pairs, rest, (keep_ref, send_ref) = refs[:n_pairs], refs[n_pairs:], refs[-2:]
    singles, own_refs = rest[:n_single], rest[n_single : n_single + 4]
    value, lse = blend([m.at[0] for m in pairs] + list(singles), head_size)
    doc = value.T
    doc_lse = jnp.broadcast_to(lse, value.shape).T
    halves = []
    for i in range(2):
        own_ref, own_lse_ref = own_refs[2 * i : 2 * i + 2]
        rows = own_ref.shape[0]
        span = slice(i * rows, (i + 1) * rows)
        own_lse = own_lse_ref[...]
        peak = jnp.maximum(doc_lse[span], own_lse)
        w_doc = jnp.exp2(doc_lse[span] - peak)
        w_own = jnp.exp2(own_lse - peak)
        halves.append((doc[span] * w_doc + own_ref[...] * w_own) / (w_doc + w_own))
    odd = lax.rem(z_ref[0], 2) == 1
    keep_ref[...] = jnp.where(odd, halves[1], halves[0]).astype(BF)
    send_ref[...] = jnp.where(odd, halves[0], halves[1]).astype(BF)


def combine(z, pairs, singles, owns, head_size, after):
    rows = pairs[0].shape[2] // 2
    vm = pl.BlockSpec(memory_space=pltpu.VMEM)
    return pl.pallas_call(
        functools.partial(combine_kernel, head_size, len(pairs), len(singles)),
        in_specs=[pl.BlockSpec(memory_space=pltpu.SMEM)]
        + [vm] * (len(pairs) + len(singles) + len(owns))
        + [pl.BlockSpec(memory_space=pl.ANY)] * len(after),
        out_specs=[vm, vm],
        out_shape=[jax.ShapeDtypeStruct((rows, head_size), BF)] * 2,
        compiler_params=params(),
        name="combine",
    )(z, *pairs, *singles, *owns, *after)


def project_kernel(n, seconds, where_ref, *refs):
    pieces, near, far, rest = refs[:n], refs[n : n + 2], refs[n + 2 : n + 4], refs[n + 4 :]
    core, z, y, x = where_ref[0], where_ref[1], where_ref[2], where_ref[3]
    held_ref = rest[0]
    if len(rest) > 1:
        held_ref = rest[-1]
        held_ref[...] = rest[0][...]
    blocks = pieces[0].shape[1] // 2
    req, head_size = pieces[0].shape[2:]
    at = 0
    for second, n_first in seconds:
        group_refs = []
        while sum(g.shape[0] for g in group_refs) < n_first:
            group_refs.append(pieces[at])
            at += 1
        accs = [None, None]
        for k in range(2):
            cols = []
            for j in range(blocks):
                parts = [g[:, k * blocks + j].reshape(-1, head_size) for g in group_refs]
                cols.append(jnp.concatenate(parts, 0) if len(parts) > 1 else parts[0])
            lhs = jnp.concatenate(cols, 1)
            for i, w_refs in enumerate((near, far)):
                part = jnp.dot(lhs, w_refs[k][...], preferred_element_type=F32)
                accs[i] = part if accs[i] is None else accs[i] + part
        for first in range(4):
            dy = jnp.where(core == 0, first, second)
            dx = jnp.where(core == 0, second, first)
            group = lax.rem(y + 4 - dy, 4)
            chip = lax.rem(x + 4 - dx, 4)
            to = lax.rem(group + 4 - z // 2, 4)
            for i in range(2):
                held_ref[to, i, chip] = accs[i][first * req : (first + 1) * req].astype(BF)
    if len(rest) > 1:
        for s, out_ref in enumerate(rest[1:-1]):
            out_ref[...] = held_ref[s]


def project(where, pieces, seconds, near, far, so_far=None):
    req = pieces[0].shape[2]
    cols = near[0].shape[1]
    part = (2, 4, req, cols)
    vm = pl.BlockSpec(memory_space=pltpu.VMEM)
    extra = [] if so_far is None else [so_far]
    whole_share = jax.ShapeDtypeStruct((4,) + part, BF)
    return pl.pallas_call(
        functools.partial(project_kernel, len(pieces), seconds),
        in_specs=[pl.BlockSpec(memory_space=pltpu.SMEM)] + [vm] * (len(pieces) + 4 + len(extra)),
        out_specs=[vm] * 4 if extra else vm,
        out_shape=[jax.ShapeDtypeStruct(part, BF)] * 4 if extra else whole_share,
        scratch_shapes=[pltpu.VMEM(whole_share.shape, BF)] if extra else [],
        compiler_params=params(),
        cost_estimate=pl.CostEstimate(flops=2 * 10**9, bytes_accessed=2**22, transcendentals=0),
        name="project",
    )(where, *pieces, *near, *far, *extra)


def total_kernel(own_ref, *refs):
    near_ref, far_ref = refs[-2:]
    total = own_ref[...]
    for ref in refs[:-2]:
        total = total + ref[...].astype(F32)
    near_ref[...] = total[0].astype(BF)
    far_ref[...] = total[1].astype(BF)


def add_up(parts):
    _, chips, req, cols = parts[0].shape
    return pl.pallas_call(
        total_kernel,
        out_shape=[jax.ShapeDtypeStruct((chips, req, cols), BF)] * 2,
        compiler_params=params(),
        name="add_up",
    )(*parts)


def slabs(where_ref, s, n_slabs):
    core, z = where_ref[0], where_ref[1]
    layer = lax.rem(z + s, 8)
    found = []
    for c in range(2):
        at_core = core if c == 0 else 1 - core
        for chip in range(n_slabs):
            pos = (layer // 2) * 2 + chip % 2
            rep = (chip // 2) * 2 + at_core
            found.append(((c, chip), (pos, rep, lax.rem(layer, 2))))
    return found


def place_kernel(steps, where_ref, *refs):
    out_ref = refs[-1]
    for s, src in zip(steps, refs[:-1]):
        for of, to in slabs(where_ref, s, src.shape[1]):
            out_ref[to] = src[of]


def place(where, pieces, steps, cols):
    return pl.pallas_call(
        functools.partial(place_kernel, steps),
        in_specs=[pl.BlockSpec(memory_space=pltpu.SMEM)] + [whole(p.shape) for p in pieces],
        out_specs=whole((8, 4, 2, 32, cols)),
        out_shape=jax.ShapeDtypeStruct((8, 4, 2, 32, cols), BF),
        compiler_params=params(),
        name="place",
    )(where, *pieces)


def place_last_kernel(step, where_ref, src_ref, _, out_ref, sems):
    copies = [
        pltpu.make_async_copy(src_ref.at[of], out_ref.at[to], sems.at[i])
        for i, (of, to) in enumerate(slabs(where_ref, step, src_ref.shape[1]))
    ]
    for copy in copies:
        copy.start()
    for copy in copies:
        copy.wait()


def place_last(where, piece, step, placed):
    hbm = pl.BlockSpec(memory_space=pl.ANY)
    return pl.pallas_call(
        functools.partial(place_last_kernel, step),
        in_specs=[
            pl.BlockSpec(memory_space=pltpu.SMEM),
            pl.BlockSpec(memory_space=pltpu.VMEM),
            hbm,
        ],
        out_specs=hbm,
        out_shape=jax.ShapeDtypeStruct(placed.shape, BF),
        scratch_shapes=[pltpu.SemaphoreType.DMA((8,))],
        input_output_aliases={2: 0},
        compiler_params=params(),
        name="place_last",
    )(where, piece, placed)


def across_x(value, dy=0):
    return lax.ppermute(value, "pos", [(p, ((p ^ 1) + 2 * dy) % 8) for p in range(8)])


def along_y(value, dy):
    return lax.ppermute(value, "pos", [(p, (p + 2 * dy) % 8) for p in range(8)])


def across_plane(value, s, first):
    pairs = []
    for pos in range(8):
        for rep in range(4):
            y, x, core = pos // 2, (rep // 2) * 2 + pos % 2, rep % 2
            if (core == 0) == first:
                y = (y + s) % 4
            else:
                x = (x + s) % 4
            pairs.append((pos * 4 + rep, (y * 2 + x % 2) * 4 + (x // 2) * 2 + core))
    return lax.ppermute(value, ("pos", "rep"), pairs)


def head_shift(value, s):
    return lax.ppermute(value, "head", [(i, (i + s) % 8) for i in range(8)])


def head_twin(value):
    return lax.ppermute(value, "head", [(i, i ^ 1) for i in range(8)])


def other_core(value):
    return lax.ppermute(value, "rep", [(i, i ^ 1) for i in range(4)])


def body(queries, doc_keys, doc_values, suffix_keys, suffix_values, suffix_len, out_weight):
    n_req, heads, head_size = queries.shape
    keys = doc_keys.reshape(-1, head_size)
    values = doc_values.reshape(-1, head_size)
    s_keys = suffix_keys.reshape(n_req, -1, head_size)
    s_values = suffix_values.reshape(n_req, -1, head_size)
    cols = out_weight.shape[1]

    beside = across_x(queries)

    half = n_req // 2
    suffix = (queries, s_keys, s_values, suffix_len)
    vt = transpose_values(values)
    pair = pair_up(queries, beside)
    arrived = {dy: along_y(pair, dy) for dy in (2, 1, 3)}
    far = [other_core(out_weight)]
    near = [out_weight, head_twin(out_weight)]
    far.append(head_twin(far[0]))

    here = doc_attention(pair, keys, vt)
    early = suffix_attention(*suffix, 0, half, (here,))
    two = doc_attention(arrived[2], keys, vt, (here, far[0], early[1]))
    two_back = along_y(two, 2)
    one = doc_attention(arrived[1], keys, vt, (two,))
    one_back = along_y(one, 3)
    three = doc_attention(arrived[3], keys, vt, (one, near[1]), split=True)
    three_back = along_y(three[0], 1)
    three_across = across_x(three[1], 1)
    passed = across_x(merge([here, two_back, one_back], head_size))
    late = suffix_attention(*suffix, half, half, (three[0],))
    z = lax.axis_index("head").astype(jnp.int32)
    keep, send = combine(
        z[None],
        [here, two_back, one_back],
        [three_back, three_across, passed],
        early + late,
        head_size,
        (far[1],),
    )

    rows = jnp.stack([keep, head_twin(send)]).reshape(2 * heads, half, head_size)
    low = jnp.stack([rows, across_plane(rows, 1, True)])
    below_low = across_plane(low, 1, False)
    high = jnp.stack([across_plane(rows, s, True) for s in (2, 3)])
    above_high = across_plane(high, 3, False)
    above_low, below_high = across_plane(low, 3, False), across_plane(high, 1, False)
    opposite = [across_plane(below_low, 1, False), across_plane(above_high, 3, False)]
    pos, rep = lax.axis_index("pos"), lax.axis_index("rep")
    where = jnp.stack([rep % 2, z, pos // 2, (rep // 2) * 2 + pos % 2]).astype(jnp.int32)
    ready = [low, high, below_low, below_high, above_low, above_high]
    share = project(where, ready, ((0, 4), (1, 4), (3, 4)), near, far)
    parts = project(where, opposite, ((2, 4),), near, far, share)
    mine, other = add_up([parts[0]] + [head_shift(parts[s], 2 * s) for s in (2, 1, 3)])
    up = down = jnp.stack([mine, other_core(other)])
    pieces = {0: up}
    for s in range(1, 5):
        up = head_shift(up, 1)
        pieces[8 - s] = up
        if s < 4:
            down = head_shift(down, 7)
            pieces[s] = down
    steps = (0, 1, 2, 3, 5, 6, 7)
    placed = place(where, [pieces[s] for s in steps], steps, cols)
    return place_last(where, pieces[4], 4, placed).reshape(-1, cols)


def solution(mesh):
    in_specs = (
        P(("pos", "rep"), "head", None),
        P("pos", "head", None),
        P("pos", "head", None),
        P(("pos", "rep"), None, "head", None),
        P(("pos", "rep"), None, "head", None),
        P(("pos", "rep")),
        P("head", ("pos", "rep")),
    )
    out_specs = P(None, ("pos", "rep"))
    return jax.shard_map(body, mesh=mesh, in_specs=in_specs, out_specs=out_specs, check_vma=False)
```

```python
import functools
import math

import jax
import jax.numpy as jnp
from jax import lax
from jax.experimental import pallas as pl
from jax.experimental.pallas import tpu as pltpu
from jax.sharding import PartitionSpec as P

BF = jnp.bfloat16
F32 = jnp.float32
LOG2E = math.log2(math.e)
VMEM = 32 * 2**20
SUFFIX_VMEM = 48 * 2**20
KEY_TILE = 512
MSG_ROWS = 144


def params(limit=VMEM):
    return pltpu.CompilerParams(vmem_limit_bytes=limit)


def whole(shape):
    return pl.BlockSpec(shape, lambda *_: (0,) * len(shape))


def transpose_kernel(v_ref, vt_ref):
    n_keys, head_size = v_ref.shape
    for j in range(n_keys // KEY_TILE):
        span = pl.ds(j * KEY_TILE, KEY_TILE)
        vt_ref[pl.ds(0, head_size), span] = v_ref[span, :].T
    vt_ref[pl.ds(head_size, 16), :] = jnp.ones((16, n_keys), BF)


def transpose_values(values):
    n_keys = values.shape[0]
    return pl.pallas_call(
        transpose_kernel,
        out_shape=jax.ShapeDtypeStruct((MSG_ROWS, n_keys), BF),
        compiler_params=params(),
        name="transpose_values",
    )(values)


def attend(q, k_ref, vt_ref, out_ref):
    n_keys, head_size = k_ref.shape
    tiles = n_keys // KEY_TILE

    def scores(j):
        return lax.dot_general(
            k_ref[pl.ds(pl.multiple_of(j * KEY_TILE, KEY_TILE), KEY_TILE), :],
            q,
            (((1,), (1,)), ((), ())),
            preferred_element_type=F32,
        )

    def mix(j, s, shift):
        weights = jnp.exp2(s - shift).astype(BF)
        span = pl.ds(pl.multiple_of(j * KEY_TILE, KEY_TILE), KEY_TILE)
        return jnp.dot(vt_ref[:, span], weights, preferred_element_type=F32)

    def emit(acc, shift):
        total = acc[head_size : head_size + 1]
        out_ref[pl.ds(0, head_size), :] = (acc[:head_size] / total).astype(BF)
        out_ref[pl.ds(head_size, 16), :] = split_lse(shift + jnp.log2(total), q.shape[0])

    s = scores(0)
    shift = s.max(0, keepdims=True)
    acc = None
    for j in range(tiles):
        ahead = scores(j + 1) if j + 1 < tiles else None
        part = mix(j, s, shift)
        acc = part if acc is None else acc + part
        s = ahead
    emit(acc, shift)
    worst = jnp.max(jnp.where(acc[head_size : head_size + 1] < 1e30, 0.0, 1.0))

    @pl.when(worst > 0.5)
    def _():
        top = lax.fori_loop(
            1, tiles, lambda j, top: jnp.maximum(top, scores(j).max(0, keepdims=True)), shift
        )
        again = lax.fori_loop(
            0, tiles, lambda j, total: total + mix(j, scores(j), top), jnp.zeros(acc.shape, F32)
        )
        emit(again, top)


def doc_kernel(split, q_ref, k_ref, vt_ref, *refs):
    for i in range(q_ref.shape[0]):
        attend(q_ref[i], k_ref, vt_ref, refs[i - 2] if split else refs[-1].at[i])


def doc_attention(chunks, keys, vt, after=(), split=False):
    n, rows, head_size = chunks.shape
    n_keys = keys.shape[0]
    work = n * rows * n_keys
    vm = pl.BlockSpec(memory_space=pltpu.VMEM)
    if split:
        out_shape = [jax.ShapeDtypeStruct((MSG_ROWS, rows), BF)] * n
    else:
        out_shape = jax.ShapeDtypeStruct((n, MSG_ROWS, rows), BF)
    return pl.pallas_call(
        functools.partial(doc_kernel, split),
        in_specs=[vm] * 3 + [pl.BlockSpec(memory_space=pl.ANY)] * len(after),
        out_specs=[vm] * n if split else vm,
        out_shape=out_shape,
        compiler_params=params(),
        cost_estimate=pl.CostEstimate(
            flops=10 * work * head_size, bytes_accessed=2**19, transcendentals=0
        ),
        name="doc_attention",
    )(chunks, keys, vt, *after)


def pair_kernel(scale, a_ref, b_ref, out_ref, held_ref):
    n_req, heads, head_size = a_ref.shape
    half = n_req // 2
    for i, ref in enumerate((a_ref, b_ref)):
        held_ref[...] = (ref[...].astype(F32) * scale).reshape(held_ref.shape)
        for parity in range(2):
            for h in range(heads):
                base = parity * half * heads
                block = held_ref[pl.ds(base + h, half, stride=heads), :]
                out_ref[i, pl.ds(base + h * half, half), :] = block.astype(BF)


def pair_up(a, b):
    n_req, heads, head_size = a.shape
    rows = n_req * heads
    return pl.pallas_call(
        functools.partial(pair_kernel, head_size ** (-0.5) * LOG2E),
        out_shape=jax.ShapeDtypeStruct((2, rows, head_size), BF),
        scratch_shapes=[pltpu.VMEM((rows, head_size), F32)],
        compiler_params=params(),
        name="pair_up",
    )(a, b)


def suffix_kernel(scale, step, base, len_ref, q_ref, k_hbm, v_hbm, *refs):
    out_ref, lse_ref, k_ref, v_ref, sems = refs[-5:]
    n_req, slots, _ = k_ref.shape
    steps = n_req // step
    copies = []
    for g in range(steps):
        span = pl.ds(g * step, step)
        source = pl.ds(base + g * step, step)
        for i, (src, dst) in enumerate(((k_hbm, k_ref), (v_hbm, v_ref))):
            copies.append(pltpu.make_async_copy(src.at[source], dst.at[span], sems.at[i, g]))
            copies[-1].start()
    lane = lax.broadcasted_iota(jnp.int32, (8, slots), 1)
    for g in range(steps):
        copies[2 * g].wait()
        copies[2 * g + 1].wait()
        scored = [
            lax.dot_general(
                q_ref[base + r], k_ref[r], (((1,), (1,)), ((), ())), preferred_element_type=F32
            )
            for r in range(g * step, (g + 1) * step)
        ]
        for i in range(step):
            r = g * step + i
            live = lane < len_ref[base + r]
            s = jnp.where(live, scored[i] * scale, -1e30)
            top = s.max(1, keepdims=True)
            terms = jnp.where(live, jnp.exp2(s - top), 0.0)
            total = terms.sum(1, keepdims=True)
            mixed = jnp.dot(terms.astype(BF), v_ref[r], preferred_element_type=F32) / total
            place = pl.ds(r, 8, stride=n_req)
            out_ref[place, :] = mixed
            lse_ref[place, :] = jnp.broadcast_to(top + jnp.log2(total), mixed.shape)


def suffix_attention(queries, keys, values, lens, base, n_req, after=()):
    _, heads, head_size = queries.shape
    slots = keys.shape[1]
    step = 8
    scale = head_size ** (-0.5) * LOG2E
    wide = jax.ShapeDtypeStruct((n_req * heads, head_size), F32)
    vm = pl.BlockSpec(memory_space=pltpu.VMEM)
    hbm = pl.BlockSpec(memory_space=pl.ANY)
    return pl.pallas_call(
        functools.partial(suffix_kernel, scale, step, base),
        in_specs=[pl.BlockSpec(memory_space=pltpu.SMEM), vm, hbm, hbm] + [hbm] * len(after),
        out_specs=[vm, vm],
        out_shape=[wide, wide],
        scratch_shapes=[
            pltpu.VMEM((n_req, slots, head_size), BF),
            pltpu.VMEM((n_req, slots, head_size), BF),
            pltpu.SemaphoreType.DMA((2, n_req // step)),
        ],
        compiler_params=params(SUFFIX_VMEM),
        cost_estimate=pl.CostEstimate(
            flops=3 * 10**9, bytes_accessed=2**21, transcendentals=2**15
        ),
        name="suffix_attention",
    )(lens, queries, keys, values, *after)


def split_lse(lse, width):
    high = lse.astype(BF).astype(F32)
    mid = (lse - high).astype(BF).astype(F32)
    low = lse - high - mid
    row = lax.broadcasted_iota(jnp.int32, (16, width), 0)
    tail = jnp.where(row == 0, high, jnp.where(row == 1, mid, jnp.where(row == 2, low, 0.0)))
    return tail.astype(BF)


def blend(msgs, head_size):
    lses = []
    for msg in msgs:
        tail = msg[pl.ds(head_size, 16), :].astype(F32)
        lses.append(tail[0:1] + tail[1:2] + tail[2:3])
    top = functools.reduce(jnp.maximum, lses)
    total = acc = None
    for msg, lse in zip(msgs, lses):
        w = jnp.exp2(lse - top)
        part = msg[pl.ds(0, head_size), :].astype(F32) * w
        total = w if total is None else total + w
        acc = part if acc is None else acc + part
    return acc / total, top + jnp.log2(total)


def merge_kernel(head_size, *refs):
    out_ref = refs[-1]
    value, lse = blend([m.at[1] for m in refs[:-1]], head_size)
    out_ref[pl.ds(0, head_size), :] = value.astype(BF)
    out_ref[pl.ds(head_size, 16), :] = split_lse(lse, value.shape[1])


def merge(msgs, head_size):
    return pl.pallas_call(
        functools.partial(merge_kernel, head_size),
        out_shape=jax.ShapeDtypeStruct(msgs[0].shape[1:], BF),
        compiler_params=params(),
        name="merge",
    )(*msgs)


def combine_kernel(head_size, n_pairs, n_single, z_ref, *refs):
    pairs, rest, (keep_ref, send_ref) = refs[:n_pairs], refs[n_pairs:], refs[-2:]
    singles, own_refs = rest[:n_single], rest[n_single : n_single + 4]
    value, lse = blend([m.at[0] for m in pairs] + list(singles), head_size)
    doc = value.T
    doc_lse = jnp.broadcast_to(lse, value.shape).T
    halves = []
    for i in range(2):
        own_ref, own_lse_ref = own_refs[2 * i : 2 * i + 2]
        rows = own_ref.shape[0]
        span = slice(i * rows, (i + 1) * rows)
        own_lse = own_lse_ref[...]
        peak = jnp.maximum(doc_lse[span], own_lse)
        w_doc = jnp.exp2(doc_lse[span] - peak)
        w_own = jnp.exp2(own_lse - peak)
        halves.append((doc[span] * w_doc + own_ref[...] * w_own) / (w_doc + w_own))
    odd = lax.rem(z_ref[0], 2) == 1
    keep_ref[...] = jnp.where(odd, halves[1], halves[0]).astype(BF)
    send_ref[...] = jnp.where(odd, halves[0], halves[1]).astype(BF)


def combine(z, pairs, singles, owns, head_size, after):
    rows = pairs[0].shape[2] // 2
    vm = pl.BlockSpec(memory_space=pltpu.VMEM)
    return pl.pallas_call(
        functools.partial(combine_kernel, head_size, len(pairs), len(singles)),
        in_specs=[pl.BlockSpec(memory_space=pltpu.SMEM)]
        + [vm] * (len(pairs) + len(singles) + len(owns))
        + [pl.BlockSpec(memory_space=pl.ANY)] * len(after),
        out_specs=[vm, vm],
        out_shape=[jax.ShapeDtypeStruct((rows, head_size), BF)] * 2,
        compiler_params=params(),
        name="combine",
    )(z, *pairs, *singles, *owns, *after)


def project_kernel(n, seconds, where_ref, *refs):
    pieces, near, far, rest = refs[:n], refs[n : n + 2], refs[n + 2 : n + 4], refs[n + 4 :]
    core, z, y, x = where_ref[0], where_ref[1], where_ref[2], where_ref[3]
    held_ref = rest[0]
    if len(rest) > 1:
        held_ref = rest[-1]
        held_ref[...] = rest[0][...]
    blocks = pieces[0].shape[1] // 2
    req, head_size = pieces[0].shape[2:]
    at = 0
    for second, n_first in seconds:
        group_refs = []
        while sum(g.shape[0] for g in group_refs) < n_first:
            group_refs.append(pieces[at])
            at += 1
        accs = [None, None]
        for k in range(2):
            cols = []
            for j in range(blocks):
                parts = [g[:, k * blocks + j].reshape(-1, head_size) for g in group_refs]
                cols.append(jnp.concatenate(parts, 0) if len(parts) > 1 else parts[0])
            lhs = jnp.concatenate(cols, 1)
            for i, w_refs in enumerate((near, far)):
                part = jnp.dot(lhs, w_refs[k][...], preferred_element_type=F32)
                accs[i] = part if accs[i] is None else accs[i] + part
        for first in range(4):
            dy = jnp.where(core == 0, first, second)
            dx = jnp.where(core == 0, second, first)
            group = lax.rem(y + 4 - dy, 4)
            chip = lax.rem(x + 4 - dx, 4)
            to = lax.rem(group + 4 - z // 2, 4)
            for i in range(2):
                held_ref[to, i, chip] = accs[i][first * req : (first + 1) * req].astype(BF)
    if len(rest) > 1:
        for s, out_ref in enumerate(rest[1:-1]):
            out_ref[...] = held_ref[s]


def project(where, pieces, seconds, near, far, so_far=None):
    req = pieces[0].shape[2]
    cols = near[0].shape[1]
    part = (2, 4, req, cols)
    vm = pl.BlockSpec(memory_space=pltpu.VMEM)
    extra = [] if so_far is None else [so_far]
    whole_share = jax.ShapeDtypeStruct((4,) + part, BF)
    return pl.pallas_call(
        functools.partial(project_kernel, len(pieces), seconds),
        in_specs=[pl.BlockSpec(memory_space=pltpu.SMEM)] + [vm] * (len(pieces) + 4 + len(extra)),
        out_specs=[vm] * 4 if extra else vm,
        out_shape=[jax.ShapeDtypeStruct(part, BF)] * 4 if extra else whole_share,
        scratch_shapes=[pltpu.VMEM(whole_share.shape, BF)] if extra else [],
        compiler_params=params(),
        cost_estimate=pl.CostEstimate(flops=2 * 10**9, bytes_accessed=2**22, transcendentals=0),
        name="project",
    )(where, *pieces, *near, *far, *extra)


def total_kernel(own_ref, *refs):
    near_ref, far_ref = refs[-2:]
    total = own_ref[...]
    for ref in refs[:-2]:
        total = total + ref[...].astype(F32)
    near_ref[...] = total[0].astype(BF)
    far_ref[...] = total[1].astype(BF)


def add_up(parts):
    _, chips, req, cols = parts[0].shape
    return pl.pallas_call(
        total_kernel,
        out_shape=[jax.ShapeDtypeStruct((chips, req, cols), BF)] * 2,
        compiler_params=params(),
        name="add_up",
    )(*parts)


def slabs(where_ref, s, n_slabs):
    core, z = where_ref[0], where_ref[1]
    layer = lax.rem(z + s, 8)
    found = []
    for c in range(2):
        at_core = core if c == 0 else 1 - core
        for chip in range(n_slabs):
            pos = (layer // 2) * 2 + chip % 2
            rep = (chip // 2) * 2 + at_core
            found.append(((c, chip), (pos, rep, lax.rem(layer, 2))))
    return found


def place_kernel(steps, where_ref, *refs):
    out_ref = refs[-1]
    for s, src in zip(steps, refs[:-1]):
        for of, to in slabs(where_ref, s, src.shape[1]):
            out_ref[to] = src[of]


def place(where, pieces, steps, cols):
    return pl.pallas_call(
        functools.partial(place_kernel, steps),
        in_specs=[pl.BlockSpec(memory_space=pltpu.SMEM)] + [whole(p.shape) for p in pieces],
        out_specs=whole((8, 4, 2, 32, cols)),
        out_shape=jax.ShapeDtypeStruct((8, 4, 2, 32, cols), BF),
        compiler_params=params(),
        name="place",
    )(where, *pieces)


def place_last_kernel(step, where_ref, src_ref, _, out_ref, sems):
    copies = [
        pltpu.make_async_copy(src_ref.at[of], out_ref.at[to], sems.at[i])
        for i, (of, to) in enumerate(slabs(where_ref, step, src_ref.shape[1]))
    ]
    for copy in copies:
        copy.start()
    for copy in copies:
        copy.wait()


def place_last(where, piece, step, placed):
    hbm = pl.BlockSpec(memory_space=pl.ANY)
    return pl.pallas_call(
        functools.partial(place_last_kernel, step),
        in_specs=[
            pl.BlockSpec(memory_space=pltpu.SMEM),
            pl.BlockSpec(memory_space=pltpu.VMEM),
            hbm,
        ],
        out_specs=hbm,
        out_shape=jax.ShapeDtypeStruct(placed.shape, BF),
        scratch_shapes=[pltpu.SemaphoreType.DMA((8,))],
        input_output_aliases={2: 0},
        compiler_params=params(),
        name="place_last",
    )(where, piece, placed)


def across_x(value, dy=0):
    return lax.ppermute(value, "pos", [(p, ((p ^ 1) + 2 * dy) % 8) for p in range(8)])


def along_y(value, dy):
    return lax.ppermute(value, "pos", [(p, (p + 2 * dy) % 8) for p in range(8)])


def across_plane(value, s, first):
    pairs = []
    for pos in range(8):
        for rep in range(4):
            y, x, core = pos // 2, (rep // 2) * 2 + pos % 2, rep % 2
            if (core == 0) == first:
                y = (y + s) % 4
            else:
                x = (x + s) % 4
            pairs.append((pos * 4 + rep, (y * 2 + x % 2) * 4 + (x // 2) * 2 + core))
    return lax.ppermute(value, ("pos", "rep"), pairs)


def head_shift(value, s):
    return lax.ppermute(value, "head", [(i, (i + s) % 8) for i in range(8)])


def head_twin(value):
    return lax.ppermute(value, "head", [(i, i ^ 1) for i in range(8)])


def other_core(value):
    return lax.ppermute(value, "rep", [(i, i ^ 1) for i in range(4)])


def body(queries, doc_keys, doc_values, suffix_keys, suffix_values, suffix_len, out_weight):
    n_req, heads, head_size = queries.shape
    keys = doc_keys.reshape(-1, head_size)
    values = doc_values.reshape(-1, head_size)
    s_keys = suffix_keys.reshape(n_req, -1, head_size)
    s_values = suffix_values.reshape(n_req, -1, head_size)
    cols = out_weight.shape[1]

    beside = across_x(queries)

    half = n_req // 2
    suffix = (queries, s_keys, s_values, suffix_len)
    vt = transpose_values(values)
    pair = pair_up(queries, beside)
    arrived = {dy: along_y(pair, dy) for dy in (2, 1, 3)}
    far = [other_core(out_weight)]
    near = [out_weight, head_twin(out_weight)]
    far.append(head_twin(far[0]))

    here = doc_attention(pair, keys, vt)
    early = suffix_attention(*suffix, 0, half, (here,))
    two = doc_attention(arrived[2], keys, vt, (here, far[0], early[1]))
    two_back = along_y(two, 2)
    one = doc_attention(arrived[1], keys, vt, (two,))
    one_back = along_y(one, 3)
    three = doc_attention(arrived[3], keys, vt, (one, near[1]), split=True)
    three_back = along_y(three[0], 1)
    three_across = across_x(three[1], 1)
    passed = across_x(merge([here, two_back, one_back], head_size))
    late = suffix_attention(*suffix, half, half, (three[0],))
    z = lax.axis_index("head").astype(jnp.int32)
    keep, send = combine(
        z[None],
        [here, two_back, one_back],
        [three_back, three_across, passed],
        early + late,
        head_size,
        (),
    )

    rows = jnp.stack([keep, head_twin(send)]).reshape(2 * heads, half, head_size)
    low = jnp.stack([rows, across_plane(rows, 1, True)])
    below_low = across_plane(low, 1, False)
    high = jnp.stack([across_plane(rows, s, True) for s in (2, 3)])
    above_high = across_plane(high, 3, False)
    above_low, below_high = across_plane(low, 3, False), across_plane(high, 1, False)
    opposite = [across_plane(below_low, 1, False), across_plane(above_high, 3, False)]
    pos, rep = lax.axis_index("pos"), lax.axis_index("rep")
    where = jnp.stack([rep % 2, z, pos // 2, (rep // 2) * 2 + pos % 2]).astype(jnp.int32)
    ready = [low, high, below_low, below_high, above_low, above_high]
    share = project(where, ready, ((0, 4), (1, 4), (3, 4)), near, far)
    parts = project(where, opposite, ((2, 4),), near, far, share)
    mine, other = add_up([parts[0]] + [head_shift(parts[s], 2 * s) for s in (2, 1, 3)])
    up = down = jnp.stack([mine, other_core(other)])
    pieces = {0: up}
    for s in range(1, 5):
        up = head_shift(up, 1)
        pieces[8 - s] = up
        if s < 4:
            down = head_shift(down, 7)
            pieces[s] = down
    steps = (0, 1, 2, 3, 5, 6, 7)
    placed = place(where, [pieces[s] for s in steps], steps, cols)
    return place_last(where, pieces[4], 4, placed).reshape(-1, cols)


def solution(mesh):
    in_specs = (
        P(("pos", "rep"), "head", None),
        P("pos", "head", None),
        P("pos", "head", None),
        P(("pos", "rep"), None, "head", None),
        P(("pos", "rep"), None, "head", None),
        P(("pos", "rep")),
        P("head", ("pos", "rep")),
    )
    out_specs = P(None, ("pos", "rep"))
    return jax.shard_map(body, mesh=mesh, in_specs=in_specs, out_specs=out_specs, check_vma=False)
```
